32 devices in a mesh: blk: 8 (over z, x), head: 4 (over y, core).
Axes of the slice: x: 2, y: 2, z: 4, core: 2. Of those that a mesh axis runs over, the one named last changes fastest.
Arguments:
- long_query: bfloat16 [1024, 4096], P('blk', 'head'), may hold values from -64 to 64
- long_new_kv: bfloat16 [2, 1024, 1024], P(None, 'blk', 'head'), may hold values from -6 to 6
- sink_kv: bfloat16 [2, 2, 4, 1024], P(None, None, None, 'head'), may hold values from -6 to 6
- window: bfloat16 [2, 8192, 1024], P(None, 'blk', 'head'), may hold values from -64 to 64
- long_len: int32 [2], replicated, may hold values from 5 to 32768, as said below
- long_offset: int32 [2], replicated, may hold values from 0 to 4095
- dec_query: bfloat16 [32, 4096], P(('blk', 'head')), may hold values from -64 to 64
- dec_new_kv: bfloat16 [32, 2, 1024], P(('blk', 'head')), may hold values from -6 to 6
- dec_cache: bfloat16 [2, 32, 512, 1024], P(None, 'blk', None, 'head'), may hold values from -64 to 64
- dec_len: int32 [32], P('blk'), may hold values from 1 to 512, as said below
- arrival_order: int32 [32], replicated, may hold values from 0 to 31, each once
Outputs:
- long_out: bfloat16 [1024, 4096], P('blk', 'head')
- dec_out: bfloat16 [32, 4096], P('blk', 'head')
The draws below stay inside these ranges and needn't reach their ends.
Inputs may be any that keep to these rules, and one draw needn't show every extreme that they name: `long_len`: one prefilling request has exactly 32768 cached tokens. `dec_len`: some decoding request has exactly 512 cached tokens.
All inputs are finite; a program needn't handle non-finite values.
Results may differ from the reference program's by a relative error of at most 0.014.
The reference program's roundings to bfloat16 on the way count: a program that leaves them out, or rounds other values in their place, can miss the bound.
Values may be sent and summed in bfloat16 or wider, within the bound.
No kernel may reach another device: no remote copies, remote signals or barrier semaphores. Data moves between devices by JAX's collectives and lax.ppermute only.
A program may use at most 64 MiB of HBM per device.

```python
import math
import jax
import jax.numpy as jnp
from jax import lax

HEADS = 32
KV_HEADS = 8
HEAD_DIM = 128
W = 4096
SINKS = 4
MAXLEN = 32768
SPAN = 512
SHORT = 512
DEC_DEV = 4
LONG = 2
QF = 4096
KVF = 1024
DEC = 32
N_BLK = 8


def rough_field(key, shape, spread):
    first_key = jax.random.fold_in(key, 0)
    base = jax.random.normal(first_key, shape, jnp.float32) * spread
    return jnp.clip(base, -64.0, 64.0)


def draw_long_query(key, part):
    return rough_field(key, (LONG * SPAN, QF), 2.5).astype(jnp.bfloat16)


def draw_window(key, part):
    return rough_field(key, (2, LONG * W, KVF), 1.0).astype(jnp.bfloat16)


def draw_dec_query(key, part):
    return rough_field(key, (DEC, QF), 2.5).astype(jnp.bfloat16)


def draw_dec_cache(key, part):
    return rough_field(key, (2, DEC, SHORT, KVF), 1.0).astype(jnp.bfloat16)


def draw_long_len(key, part):
    first_key, second_key = jax.random.split(key, 2)
    lengths = jax.random.randint(first_key, (LONG,), SINKS + 1, MAXLEN + 1, dtype=jnp.int32)
    chosen = jax.random.randint(second_key, (), 0, LONG, dtype=jnp.int32)
    return lengths.at[chosen].set(MAXLEN)


def draw_dec_len(key, part):
    first_key, second_key = jax.random.split(key, 2)
    lengths = jax.random.randint(first_key, (DEC,), 1, SHORT + 1, dtype=jnp.int32)
    chosen = jax.random.randint(second_key, (), 0, DEC, dtype=jnp.int32)
    return lengths.at[chosen].set(SHORT)


def steps_of(rng, extent, cuts, smallest, top_value):
    loudness, own = 1.0, jax.random.fold_in(rng, 6)
    for position, blocks in cuts:
        heights = jnp.exp(jax.random.uniform(jax.random.fold_in(own, position), (blocks,), jnp.float32, smallest / len(cuts), top_value / len(cuts)))
        loudness = loudness * jnp.repeat(heights, extent[position] // blocks).reshape([-1 if axis == position else 1 for axis in range(len(extent))])
    return loudness


def noise(key, shape, width, reach, shards=(), kind=jnp.bfloat16):
    drawn = jax.random.normal(key, shape, jnp.float32) * width
    if len(shards) > 0:
        drawn = steps_of(key, shape, shards, -0.22, 0.18) * drawn
    return jnp.clip(drawn, min=-reach, max=reach).astype(kind)


def setup_inputs(seed: int = 0) -> dict:
    key_of = jax.random.split(jax.random.key(seed), 12)
    return {
        "long_query": draw_long_query(jax.random.fold_in(key_of[11], 71), 0),
        "long_new_kv": noise(key_of[1], (2, LONG * SPAN, KVF), 1.0, 6.0, ((1, 8), (2, 4))),
        "sink_kv": noise(key_of[2], (2, LONG, SINKS, KVF), 1.5, 6.0, ((3, 4),)),
        "window": draw_window(jax.random.fold_in(key_of[11], 71), 0),
        "long_len": draw_long_len(jax.random.fold_in(key_of[11], 71), 0),
        "long_offset": jax.random.randint(key_of[5], (LONG,), 0, W).astype(jnp.int32),
        "dec_query": draw_dec_query(jax.random.fold_in(key_of[11], 71), 0),
        "dec_new_kv": noise(key_of[7], (DEC, 2, KVF), 1.0, 6.0, ((0, 32),)),
        "dec_cache": draw_dec_cache(jax.random.fold_in(key_of[11], 71), 0),
        "dec_len": draw_dec_len(jax.random.fold_in(key_of[11], 71), 0),
        "arrival_order": jax.random.permutation(key_of[10], DEC).astype(jnp.int32),
    }


MASKED_SCORE = -1e+30

def rotate(vectors, positions):
    halfway = HEAD_DIM // 2
    frequency = 10000.0 ** (-(jnp.arange(halfway, dtype=jnp.float32) * 2.0 / HEAD_DIM))
    angles = positions.astype(jnp.float32)[:, None] * frequency[None, :]
    cosine = jnp.cos(angles)[:, None, :]
    sine_part = jnp.sin(angles)[:, None, :]
    first_half = vectors[..., :halfway]
    second_half = vectors[..., halfway:]
    return jnp.concatenate([first_half * cosine - second_half * sine_part, second_half * cosine + first_half * sine_part], axis=-1)

def finish(scores, visible, value_rows, pattern):
    scores = jnp.where(visible, scores, MASKED_SCORE)
    row_top = lax.optimization_barrier(jnp.max(scores, axis=-1, keepdims=True))
    weights = jnp.exp(scores - row_top)
    row_total = lax.optimization_barrier(jnp.sum(weights, axis=-1))
    rounded = lax.optimization_barrier(weights.astype(jnp.bfloat16))
    mixed_out = jnp.einsum(pattern, rounded.astype(jnp.float32), value_rows.astype(jnp.float32))
    return mixed_out / row_total[..., None]

def reference(long_query, long_new_kv, sink_kv, window, long_len, long_offset, dec_query, dec_new_kv, dec_cache, dec_len, arrival_order):
    group_size = HEADS // KV_HEADS
    score_scale = 1.0 / math.sqrt(HEAD_DIM)
    long_parts = []
    for request in range(LONG):
        first_row = request * SPAN
        first_slot = request * W
        length = long_len[request]
        steps_in = jnp.arange(SPAN, dtype=jnp.int32)
        positions = length + steps_in
        queries = rotate(long_query[first_row:first_row + SPAN].reshape(SPAN, HEADS, HEAD_DIM).astype(jnp.float32), positions).astype(jnp.bfloat16)
        queries = queries.reshape(SPAN, KV_HEADS, group_size, HEAD_DIM)
        span_key = rotate(long_new_kv[0, first_row:first_row + SPAN].reshape(SPAN, KV_HEADS, HEAD_DIM).astype(jnp.float32), positions).astype(jnp.bfloat16)
        span_value = long_new_kv[1, first_row:first_row + SPAN].reshape(SPAN, KV_HEADS, HEAD_DIM)
        key_rows = jnp.concatenate([sink_kv[0, request].reshape(SINKS, KV_HEADS, HEAD_DIM), window[0, first_slot:first_slot + W].reshape(W, KV_HEADS, HEAD_DIM), span_key], axis=0)
        value_rows = jnp.concatenate([sink_kv[1, request].reshape(SINKS, KV_HEADS, HEAD_DIM), window[1, first_slot:first_slot + W].reshape(W, KV_HEADS, HEAD_DIM), span_value], axis=0)
        filled = jnp.minimum(length - SINKS, W)
        slot_age = jnp.mod(jnp.arange(W, dtype=jnp.int32) - long_offset[request], W)
        in_window = (slot_age[None, :] < filled) & (slot_age[None, :] > steps_in[:, None] + filled - W)
        causal = steps_in[None, :] <= steps_in[:, None]
        visible = jnp.concatenate([jnp.ones((SPAN, SINKS), dtype=bool), in_window, causal], axis=1)
        scores = jnp.einsum('nkgd,mkd->nkgm', queries.astype(jnp.float32), key_rows.astype(jnp.float32)) * score_scale
        mixed_out = finish(scores, visible[:, None, None, :], value_rows, 'nkgm,mkd->nkgd')
        long_parts.append(mixed_out.reshape(SPAN, HEADS * HEAD_DIM).astype(jnp.bfloat16))
    long_out = jnp.concatenate(long_parts, axis=0)
    inverse = jnp.argsort(arrival_order).astype(jnp.int32)
    query_rows = dec_query[inverse]
    new_rows = dec_new_kv[inverse]
    dec_q = rotate(query_rows.reshape(DEC, HEADS, HEAD_DIM).astype(jnp.float32), dec_len).astype(jnp.bfloat16)
    dec_q = dec_q.reshape(DEC, KV_HEADS, group_size, HEAD_DIM)
    dec_key = rotate(new_rows[:, 0].reshape(DEC, KV_HEADS, HEAD_DIM).astype(jnp.float32), dec_len).astype(jnp.bfloat16)
    cache_keys = jnp.concatenate([dec_cache[0].reshape(DEC, SHORT, KV_HEADS, HEAD_DIM), dec_key[:, None]], axis=1)
    cache_values = jnp.concatenate([dec_cache[1].reshape(DEC, SHORT, KV_HEADS, HEAD_DIM), new_rows[:, 1].reshape(DEC, 1, KV_HEADS, HEAD_DIM)], axis=1)
    slot_ids = jnp.arange(SHORT + 1, dtype=jnp.int32)
    visible = (slot_ids[None, :] < dec_len[:, None]) | (slot_ids[None, :] == SHORT)

    def decode_block(operands):
        block_q, block_keys, block_values, block_visible = operands
        scores = jnp.einsum('nkgd,nmkd->nkgm', block_q.astype(jnp.float32), block_keys.astype(jnp.float32)) * score_scale
        return finish(scores, block_visible[:, None, None, :], block_values, 'nkgm,nmkd->nkgd')
    blocks = lax.map(decode_block, (dec_q.reshape(N_BLK, DEC_DEV, KV_HEADS, group_size, HEAD_DIM), cache_keys.reshape(N_BLK, DEC_DEV, SHORT + 1, KV_HEADS, HEAD_DIM), cache_values.reshape(N_BLK, DEC_DEV, SHORT + 1, KV_HEADS, HEAD_DIM), visible.reshape(N_BLK, DEC_DEV, SHORT + 1)))
    dec_out = blocks.reshape(DEC, HEADS * HEAD_DIM).astype(jnp.bfloat16)
    return (long_out, dec_out)
```

```python
import functools
import math

import jax
import jax.numpy as jnp
from jax import lax
from jax.experimental import pallas as pl
from jax.experimental.pallas import tpu as pltpu
from jax.sharding import PartitionSpec as P

D = 128
W = 4096
SINKS = 4
SPAN = 512
PAD_PARTS = 16
HIDDEN = -1e30
LOG2_SCALE = math.log2(math.e) / math.sqrt(D)
VMEM = pltpu.CompilerParams(vmem_limit_bytes=24 * 1024 * 1024)


def turn(x, cosine, sine):
    return x * cosine + pltpu.roll(x, D // 2, 1) * sine


def split_three(x):
    high = x.astype(jnp.bfloat16)
    rest = x - high.astype(jnp.float32)
    middle = rest.astype(jnp.bfloat16)
    low = (rest - middle.astype(jnp.float32)).astype(jnp.bfloat16)
    return high, middle, low


def angle_tables(length, first_step, frequency):
    half = D // 2
    line = lax.broadcasted_iota(jnp.int32, (half, D), 0)
    lane = lax.broadcasted_iota(jnp.int32, (half, D), 1)
    low = lane < half
    position = length + first_step + line + jnp.where(low, 0, half)
    angle = position.astype(jnp.float32) * frequency
    cosine, sine = jnp.cos(angle), jnp.sin(angle)
    cosine_r, sine_r = pltpu.roll(cosine, half, 1), pltpu.roll(sine, half, 1)
    cosines = [jnp.where(low, cosine, cosine_r), jnp.where(low, cosine_r, cosine)]
    sines = [jnp.where(low, -sine, sine_r), jnp.where(low, -sine_r, sine)]
    return jnp.concatenate(cosines, axis=0), jnp.concatenate(sines, axis=0)


def whereabouts(rows):
    members = SPAN // rows
    blk = lax.axis_index("blk")
    return blk // members, lax.rem(blk, members)


def spread_kernel(query, new_kv, *pieces):
    head_at = lax.axis_index("head")
    width = query.shape[1] // len(pieces)
    kv_width = new_kv.shape[2] // len(pieces)

    def lines(ref, size, at):
        found = ref[:, pl.ds(pl.multiple_of(at * size, D), size)].astype(jnp.float32)
        return [
            found[line : line + 1, low : low + D]
            for line in range(found.shape[0])
            for low in range(0, size, D)
        ]

    for distance, piece in enumerate(pieces):
        at = head_at ^ distance
        found = lines(query, width, at) + lines(new_kv.at[0], kv_width, at)
        found.append(jnp.zeros((PAD_PARTS - len(found), D), jnp.float32))
        piece[...] = jnp.concatenate(found, axis=0).astype(piece.dtype)


def prepare_kernel(
    lengths, new_kv, sinks, values, frequency, near_keys, values_t, cosines, sines, pad
):
    rows = new_kv.shape[1]
    slots = values.shape[1]
    request, place = whereabouts(rows)
    for part in range(cosines.shape[0]):
        first_step = (place ^ part) * rows
        for low in range(0, rows, D):
            lines = slice(low, low + D)
            cosines[part, lines], sines[part, lines] = angle_tables(
                lengths[request], first_step + low, frequency[...]
            )
    for head in range(new_kv.shape[2] // D):
        lanes = slice(head * D, (head + 1) * D)
        key = turn(new_kv[0, :, lanes].astype(jnp.float32), cosines[0], sines[0])
        near_keys[:rows, lanes] = key.astype(jnp.bfloat16)
    for kind in range(2):
        pad[...] = jnp.zeros_like(pad)
        pad[:SINKS, :] = sinks[kind, request].astype(jnp.float32)
        if kind == 0:
            near_keys[rows:, :] = pad[...].astype(jnp.bfloat16)
        else:
            values_t[:, slots + rows :] = pad[...].T.astype(jnp.bfloat16)
    values_t[:, :slots] = values[0].T
    values_t[:, slots : slots + rows] = new_kv[1].T


def attend_kernel(
    part, own, lengths, offsets, query, keys, near_keys, values_t, cosine, sine, out, scores, weights
):
    rows = query.shape[0]
    slots = keys.shape[1]
    kv_heads = keys.shape[2] // D
    group = query.shape[1] // D // kv_heads
    request, place = whereabouts(rows)
    offset, first_slot = offsets[request], place * slots
    filled = jnp.minimum(lengths[request] - SINKS, W)
    first_step = (place ^ part) * rows
    step = first_step + lax.broadcasted_iota(jnp.int32, (D, rows), 1)
    index = lax.broadcasted_iota(jnp.int32, (D, rows), 0)
    masks = []
    for low in range(0, slots, D):
        age = (first_slot + low - offset + index) & (W - 1)
        limit = jnp.where(age < filled, age - filled + W, -1)
        masks.append(jnp.where(limit > step, 0.0, HIDDEN))
    for low in range(0, rows, D):
        masks.append(jnp.where(place * rows + low + index <= step, 0.0, HIDDEN))
    if own:
        masks.append(jnp.where(index < SINKS, 0.0, HIDDEN))
    total = len(masks) * D
    logs = []
    for kv in range(kv_heads):
        lanes = slice(kv * D, (kv + 1) * D)
        turned = []
        for head in range(kv * group, (kv + 1) * group):
            x = query[:, head * D : (head + 1) * D].astype(jnp.float32)
            turned.append(turn(x, cosine[0], sine[0]).astype(jnp.bfloat16))
        block = jnp.concatenate(turned, axis=0)
        top = None
        for number, mask in enumerate(masks):
            low = number * D
            if low < slots:
                chunk = keys[0, low : low + D, lanes]
            else:
                chunk = near_keys[low - slots : low - slots + D, lanes]
            s = lax.dot_general(
                chunk, block, (((1,), (1,)), ((), ())), preferred_element_type=jnp.float32
            )
            s = s + jnp.concatenate([mask] * group, axis=1)
            scores[low : low + D, :] = s
            peak = jnp.max(s.reshape(D // 8, 8, group * rows), axis=0)
            top = peak if top is None else jnp.maximum(top, peak)
        top = jnp.max(top, axis=0, keepdims=True)
        mass = jnp.zeros((8, group * rows), jnp.float32)
        for low in range(0, total, D):
            w = jnp.exp2((scores[low : low + D, :] - top) * LOG2_SCALE)
            mass = mass + jnp.sum(w.reshape(D // 8, 8, group * rows), axis=0)
            weights[low : low + D, :] = w.astype(jnp.bfloat16)
        mass = jnp.sum(mass, axis=0, keepdims=True)
        mix = jnp.dot(
            values_t[lanes, :total], weights[:total, :], preferred_element_type=jnp.float32
        )
        mix = mix * (1.0 / mass)
        log = top * LOG2_SCALE + jnp.log2(mass)
        for j in range(group):
            head = kv * group + j
            out[head * D : (head + 1) * D, :] = mix[:, j * rows : (j + 1) * rows].astype(out.dtype)
            logs.append(log[:, j * rows : (j + 1) * rows])
    log = jnp.concatenate(logs, axis=0)
    heads = len(logs)
    if own:
        out[heads * D :, :] = log
    else:
        pieces = [p.astype(jnp.float32) for p in split_three(log)]
        pieces.append(jnp.zeros_like(log))
        out[heads * D :, :] = jnp.concatenate(pieces, axis=0).astype(out.dtype)


def combine_kernel(own, first, second, third, out):
    rows = out.shape[0]
    heads = out.shape[1] // D
    logs = [own[heads * D :, :]]
    for other in (first, second, third):
        p = other[heads * D :, :].astype(jnp.float32)
        logs.append(p[:heads] + p[heads : 2 * heads] + p[2 * heads : 3 * heads])
    top = functools.reduce(jnp.maximum, logs)
    shares = [jnp.exp2(log - top) for log in logs]
    scale = 1.0 / sum(shares)
    shares = [share * scale for share in shares]
    for head in range(heads):
        lines = slice(head * D, (head + 1) * D)
        mix = own[lines, :] * shares[0][head : head + 1, :]
        for other, share in zip((first, second, third), shares[1:]):
            mix = mix + other[lines, :].astype(jnp.float32) * share[head : head + 1, :]
        out[:, lines] = mix.T.astype(out.dtype)


def decode_kernel(lengths, arrivals, *refs):
    near, (cache, frequency, out, mixed) = refs[: len(refs) - 4], refs[len(refs) - 4 :]
    count = cache.shape[1]
    slots = cache.shape[2]
    kv_heads = cache.shape[3] // D
    heads = out.shape[1] // D
    group = heads // kv_heads
    blk, head_at = lax.axis_index("blk"), lax.axis_index("head")
    head_count = lax.axis_size("head")
    members = len(near)

    def look(i, found):
        owner = arrivals[i] - blk * count
        return tuple(jnp.where(owner == n, i, was) for n, was in enumerate(found))

    found = lax.fori_loop(
        0, arrivals.shape[0], look, (jnp.int32(0),) * count, unroll=8
    )
    head_of = lax.broadcasted_iota(jnp.int32, (heads, D), 0) // group
    for n in range(count):
        away = (found[n] // head_count) ^ blk
        line = (away // members) * head_count + (lax.rem(found[n], head_count) ^ head_at)
        lines = pl.ds(pl.multiple_of(line * PAD_PARTS, PAD_PARTS), PAD_PARTS)
        x = near[0][lines, :]
        for part in range(1, members):
            x = jnp.where(lax.rem(away, members) == part, near[part][lines, :], x)
        x = x.astype(jnp.float32)
        angle = lengths[n].astype(jnp.float32) * frequency[...]
        lane = lax.broadcasted_iota(jnp.int32, angle.shape, 1)
        sine = jnp.sin(angle)
        turned = turn(x, jnp.cos(angle), jnp.where(lane < D // 2, -sine, sine))
        turned = turned.astype(jnp.bfloat16).astype(jnp.float32)
        q = turned[:heads]
        wide = [jnp.where(head_of == kv, q, 0.0) for kv in range(kv_heads)]
        wide = jnp.concatenate(wide, axis=1).astype(jnp.bfloat16)
        new_key = jnp.zeros((heads, D), jnp.float32)
        new_value = jnp.zeros((heads, D), jnp.float32)
        for kv in range(kv_heads):
            key = turned[heads + kv : heads + kv + 1]
            value = x[heads + kv_heads + kv : heads + kv_heads + kv + 1]
            new_key = jnp.where(head_of == kv, key, new_key)
            new_value = jnp.where(head_of == kv, value, new_value)
        s = lax.dot_general(
            wide, cache[0, n], (((1,), (1,)), ((), ())), preferred_element_type=jnp.float32
        )
        slot = lax.broadcasted_iota(jnp.int32, (heads, slots), 1)
        s = jnp.where(slot < lengths[n], s, HIDDEN)
        own_s = jnp.sum(q * new_key, axis=1, keepdims=True)
        top = jnp.maximum(jnp.max(s, axis=1, keepdims=True), own_s)
        w = jnp.exp2((s - top) * LOG2_SCALE)
        own_w = jnp.exp2((own_s - top) * LOG2_SCALE)
        mass = jnp.sum(w, axis=1, keepdims=True) + own_w
        mix = jnp.dot(w.astype(jnp.bfloat16), cache[1, n], preferred_element_type=jnp.float32)
        picked = own_w.astype(jnp.bfloat16).astype(jnp.float32) * new_value
        for kv in range(kv_heads):
            picked = picked + jnp.where(head_of == kv, mix[:, kv * D : (kv + 1) * D], 0.0)
        picked = picked / mass
        for head in range(heads):
            mixed[n : n + 1, head * D : (head + 1) * D] = picked[head : head + 1, :]
    out[...] = mixed[...].astype(out.dtype)


def whole(array):
    return pl.BlockSpec(array.shape, lambda i, rank=array.ndim: (0,) * rank)


def exchange(block, axis, distance):
    count = lax.axis_size(axis)
    return lax.ppermute(block, axis, [(i, i ^ distance) for i in range(count)])


SCALARS = pl.BlockSpec(memory_space=pltpu.SMEM)


def shards(
    long_query,
    long_new_kv,
    sink_kv,
    window,
    long_len,
    long_offset,
    dec_query,
    dec_new_kv,
    dec_cache,
    dec_len,
    arrival_order,
):
    blk_count, head_count = lax.axis_size("blk"), lax.axis_size("head")
    rows, features = long_query.shape
    heads = features // D
    kv_width = long_new_kv.shape[2]
    kv_heads = kv_width // D
    group = heads // kv_heads
    slots = window.shape[1]
    members = SPAN // rows
    own_count = dec_cache.shape[1]

    queries = [long_query] + [exchange(long_query, "blk", part) for part in range(1, members)]

    half = jnp.arange(D, dtype=jnp.int32) % (D // 2)
    frequency = (10000.0 ** (-(half.astype(jnp.float32) * 2.0 / D))).reshape(1, D)

    def call(kernel, out_shape, operands, specs, scratch):
        return pl.pallas_call(
            kernel,
            grid=(1,),
            in_specs=specs,
            out_specs=jax.tree.map(whole, out_shape),
            out_shape=out_shape,
            scratch_shapes=scratch,
            compiler_params=VMEM,
        )(*operands)

    pieces = call(
        spread_kernel,
        (jax.ShapeDtypeStruct((PAD_PARTS, D), jnp.bfloat16),) * head_count,
        (dec_query, dec_new_kv),
        [whole(dec_query), whole(dec_new_kv)],
        [],
    )
    arrived = jnp.concatenate(
        [exchange(piece, "head", r) if r else piece for r, piece in enumerate(pieces)], axis=0
    )
    distance = members
    while distance < blk_count:
        arrived = jnp.concatenate([arrived, exchange(arrived, "blk", distance)], axis=0)
        distance *= 2
    near = [arrived] + [exchange(arrived, "blk", part) for part in range(1, members)]

    table = lambda part: pl.BlockSpec((1, rows, D), lambda i: (part, 0, 0))
    near_keys, values_t, cosines, sines = call(
        prepare_kernel,
        (
            jax.ShapeDtypeStruct((rows + D, kv_width), jnp.bfloat16),
            jax.ShapeDtypeStruct((kv_width, slots + rows + D), jnp.bfloat16),
            jax.ShapeDtypeStruct((members, rows, D), jnp.float32),
            jax.ShapeDtypeStruct((members, rows, D), jnp.float32),
        ),
        (long_len, long_new_kv, sink_kv, window, frequency),
        [
            SCALARS,
            whole(long_new_kv),
            whole(sink_kv),
            pl.BlockSpec((1, slots, kv_width), lambda i: (1, 0, 0)),
            whole(frequency),
        ],
        [pltpu.VMEM((D, kv_width), jnp.float32)],
    )

    def attend(part):
        own = part == 0
        total = slots + rows + D
        if own:
            out = jax.ShapeDtypeStruct((features + heads, rows), jnp.float32)
        else:
            out = jax.ShapeDtypeStruct((features + 4 * heads, rows), jnp.bfloat16)
        return call(
            functools.partial(attend_kernel, part, own),
            out,
            (long_len, long_offset, queries[part], window, near_keys, values_t, cosines, sines),
            [
                SCALARS,
                SCALARS,
                whole(queries[part]),
                pl.BlockSpec((1, slots, kv_width), lambda i: (0, 0, 0)),
                whole(near_keys),
                whole(values_t),
                table(part),
                table(part),
            ],
            [
                pltpu.VMEM((total, group * rows), jnp.float32),
                pltpu.VMEM((total, group * rows), jnp.bfloat16),
            ],
        )

    mine = attend(0)
    others = [exchange(attend(part), "blk", part) for part in range(1, members)]
    long_out = call(
        combine_kernel,
        jax.ShapeDtypeStruct((rows, features), jnp.bfloat16),
        (mine, *others),
        [whole(mine)] + [whole(other) for other in others],
        [],
    )
    dec_out = call(
        decode_kernel,
        jax.ShapeDtypeStruct((own_count, features), jnp.bfloat16),
        (dec_len, arrival_order, *near, dec_cache, frequency),
        [SCALARS, SCALARS] + [whole(a) for a in (*near, dec_cache, frequency)],
        [
            pltpu.VMEM((own_count, features), jnp.float32),
        ],
    )
    return (long_out, dec_out)


def solution(mesh):
    in_specs = (
        P("blk", "head"),
        P(None, "blk", "head"),
        P(None, None, None, "head"),
        P(None, "blk", "head"),
        P(),
        P(),
        P(("blk", "head"), None),
        P(("blk", "head"), None, None),
        P(None, "blk", None, "head"),
        P("blk"),
        P(),
    )
    out_specs = (P("blk", "head"), P("blk", "head"))
    return jax.shard_map(shards, mesh=mesh, in_specs=in_specs, out_specs=out_specs, check_vma=False)
```

```python
import functools
import math

import jax
import jax.numpy as jnp
from jax import lax
from jax.experimental import pallas as pl
from jax.experimental.pallas import tpu as pltpu
from jax.sharding import PartitionSpec as P

D = 128
W = 4096
SINKS = 4
SPAN = 512
PAD_PARTS = 16
HIDDEN = -1e30
LOG2_SCALE = math.log2(math.e) / math.sqrt(D)
VMEM = pltpu.CompilerParams(vmem_limit_bytes=24 * 1024 * 1024)


def turn(x, cosine, sine):
    return x * cosine + pltpu.roll(x, D // 2, 1) * sine


def split_three(x):
    high = x.astype(jnp.bfloat16)
    rest = x - high.astype(jnp.float32)
    middle = rest.astype(jnp.bfloat16)
    low = (rest - middle.astype(jnp.float32)).astype(jnp.bfloat16)
    return high, middle, low


def angle_tables(length, first_step, frequency):
    half = D // 2
    line = lax.broadcasted_iota(jnp.int32, (half, D), 0)
    lane = lax.broadcasted_iota(jnp.int32, (half, D), 1)
    low = lane < half
    position = length + first_step + line + jnp.where(low, 0, half)
    angle = position.astype(jnp.float32) * frequency
    cosine, sine = jnp.cos(angle), jnp.sin(angle)
    cosine_r, sine_r = pltpu.roll(cosine, half, 1), pltpu.roll(sine, half, 1)
    cosines = [jnp.where(low, cosine, cosine_r), jnp.where(low, cosine_r, cosine)]
    sines = [jnp.where(low, -sine, sine_r), jnp.where(low, -sine_r, sine)]
    return jnp.concatenate(cosines, axis=0), jnp.concatenate(sines, axis=0)


def whereabouts(rows):
    members = SPAN // rows
    blk = lax.axis_index("blk")
    return blk // members, lax.rem(blk, members)


def fetch(*pairs):
    copies = [pltpu.make_async_copy(*pair) for pair in pairs]
    for copy in copies:
        copy.start()
    return copies


def spread_kernel(query_far, new_kv_far, *refs):
    pieces, (query, new_kv, arrived) = refs[:-3], refs[-3:]
    for copy in fetch(
        (query_far, query, arrived.at[0]), (new_kv_far, new_kv, arrived.at[1])
    ):
        copy.wait()
    head_at = lax.axis_index("head")
    width = query.shape[1] // len(pieces)
    kv_width = new_kv.shape[2] // len(pieces)

    def lines(ref, size, at):
        found = ref[:, pl.ds(pl.multiple_of(at * size, D), size)].astype(jnp.float32)
        return [
            found[line : line + 1, low : low + D]
            for line in range(found.shape[0])
            for low in range(0, size, D)
        ]

    for distance, piece in enumerate(pieces):
        at = head_at ^ distance
        found = lines(query, width, at) + lines(new_kv.at[0], kv_width, at)
        found.append(jnp.zeros((PAD_PARTS - len(found), D), jnp.float32))
        piece[...] = jnp.concatenate(found, axis=0).astype(piece.dtype)


def prepare_kernel(
    lengths_far,
    offsets_far,
    new_kv_far,
    sinks_far,
    window_far,
    frequency,
    keys,
    values_t,
    cosines,
    sines,
    biases,
    lengths,
    offsets,
    new_kv,
    sinks,
    values,
    pad,
    arrived,
):
    rows = new_kv.shape[1]
    slots = values.shape[0]
    request, place = whereabouts(rows)
    scalars = fetch(
        (lengths_far, lengths, arrived.at[0]),
        (offsets_far, offsets, arrived.at[1]),
    )
    arrays = fetch(
        (new_kv_far, new_kv, arrived.at[2]),
        (sinks_far.at[:, request], sinks, arrived.at[3]),
        (window_far.at[1], values, arrived.at[4]),
        (window_far.at[0], keys.at[:slots], arrived.at[5]),
    )
    for copy in scalars:
        copy.wait()
    length, offset = lengths[request], offsets[request]
    filled = jnp.minimum(length - SINKS, W)
    for part in range(cosines.shape[0]):
        first_step = (place ^ part) * rows
        for low in range(0, rows, D):
            lines = slice(low, low + D)
            cosines[part, lines], sines[part, lines] = angle_tables(
                length, first_step + low, frequency[...]
            )
    index = lax.broadcasted_iota(jnp.int32, (D, rows), 0)
    step = lax.broadcasted_iota(jnp.int32, (D, rows), 1)
    for low in range(0, slots, D):
        age = (place * slots + low - offset + index) & (W - 1)
        limit = jnp.where(age < filled, age - filled + W, -1)
        for part in range(biases.shape[0]):
            seen = limit > (place ^ part) * rows + step
            biases[part, low : low + D] = jnp.where(seen, 0.0, HIDDEN)
    for low in range(0, rows, D):
        for part in range(biases.shape[0]):
            seen = place * rows + low + index <= (place ^ part) * rows + step
            biases[part, slots + low : slots + low + D] = jnp.where(seen, 0.0, HIDDEN)
    for part in range(biases.shape[0]):
        seen = index < (SINKS if part == 0 else 0)
        biases[part, slots + rows :] = jnp.where(seen, 0.0, HIDDEN)
    for copy in arrays:
        copy.wait()
    for head in range(new_kv.shape[2] // D):
        lanes = slice(head * D, (head + 1) * D)
        key = turn(new_kv[0, :, lanes].astype(jnp.float32), cosines[0], sines[0])
        keys[slots : slots + rows, lanes] = key.astype(jnp.bfloat16)
    for kind in range(2):
        pad[...] = jnp.zeros_like(pad)
        pad[:SINKS, :] = sinks[kind].astype(jnp.float32)
        if kind == 0:
            keys[slots + rows :, :] = pad[...].astype(jnp.bfloat16)
        else:
            values_t[:, slots + rows :] = pad[...].T.astype(jnp.bfloat16)
    values_t[:, :slots] = values[...].T
    values_t[:, slots : slots + rows] = new_kv[1].T


def attend_kernel(part, own, query, keys, values_t, cosine, sine, bias, out, scores, weights):
    rows = query.shape[0]
    kv_heads = keys.shape[1] // D
    group = query.shape[1] // D // kv_heads
    total = keys.shape[0] if own else keys.shape[0] - D
    logs = []
    for kv in range(kv_heads):
        lanes = slice(kv * D, (kv + 1) * D)
        turned = []
        for head in range(kv * group, (kv + 1) * group):
            x = query[:, head * D : (head + 1) * D].astype(jnp.float32)
            turned.append(turn(x, cosine[part], sine[part]).astype(jnp.bfloat16))
        block = jnp.concatenate(turned, axis=0)
        top = None
        for low in range(0, total, D):
            chunk = keys[low : low + D, lanes]
            mask = bias[part, low : low + D]
            s = lax.dot_general(
                chunk, block, (((1,), (1,)), ((), ())), preferred_element_type=jnp.float32
            )
            s = s + jnp.concatenate([mask] * group, axis=1)
            scores[low : low + D, :] = s
            peak = jnp.max(s.reshape(D // 8, 8, group * rows), axis=0)
            top = peak if top is None else jnp.maximum(top, peak)
        top = jnp.max(top, axis=0, keepdims=True)
        mass = jnp.zeros((8, group * rows), jnp.float32)
        for low in range(0, total, D):
            w = jnp.exp2((scores[low : low + D, :] - top) * LOG2_SCALE)
            mass = mass + jnp.sum(w.reshape(D // 8, 8, group * rows), axis=0)
            weights[low : low + D, :] = w.astype(jnp.bfloat16)
        mass = jnp.sum(mass, axis=0, keepdims=True)
        mix = jnp.dot(
            values_t[lanes, :total], weights[:total, :], preferred_element_type=jnp.float32
        )
        mix = mix * (1.0 / mass)
        log = top * LOG2_SCALE + jnp.log2(mass)
        for j in range(group):
            head = kv * group + j
            out[head * D : (head + 1) * D, :] = mix[:, j * rows : (j + 1) * rows].astype(out.dtype)
            logs.append(log[:, j * rows : (j + 1) * rows])
    log = jnp.concatenate(logs, axis=0)
    heads = len(logs)
    if own:
        out[heads * D :, :] = log
    else:
        pieces = [p.astype(jnp.float32) for p in split_three(log)]
        pieces.append(jnp.zeros_like(log))
        out[heads * D :, :] = jnp.concatenate(pieces, axis=0).astype(out.dtype)


def combine_kernel(own, first, second, third, out):
    rows = out.shape[0]
    heads = out.shape[1] // D
    logs = [own[heads * D :, :]]
    for other in (first, second, third):
        p = other[heads * D :, :].astype(jnp.float32)
        logs.append(p[:heads] + p[heads : 2 * heads] + p[2 * heads : 3 * heads])
    top = functools.reduce(jnp.maximum, logs)
    shares = [jnp.exp2(log - top) for log in logs]
    scale = 1.0 / sum(shares)
    shares = [share * scale for share in shares]
    for head in range(heads):
        lines = slice(head * D, (head + 1) * D)
        mix = own[lines, :] * shares[0][head : head + 1, :]
        for other, share in zip((first, second, third), shares[1:]):
            mix = mix + other[lines, :].astype(jnp.float32) * share[head : head + 1, :]
        out[:, lines] = mix.T.astype(out.dtype)


def decode_kernel(lengths, arrivals, *refs):
    near, (cache, frequency, out, mixed) = refs[: len(refs) - 4], refs[len(refs) - 4 :]
    count = cache.shape[1]
    slots = cache.shape[2]
    kv_heads = cache.shape[3] // D
    heads = out.shape[1] // D
    group = heads // kv_heads
    blk, head_at = lax.axis_index("blk"), lax.axis_index("head")
    head_count = lax.axis_size("head")
    members = len(near)

    def look(i, found):
        owner = arrivals[i] - blk * count
        return tuple(jnp.where(owner == n, i, was) for n, was in enumerate(found))

    found = lax.fori_loop(
        0, arrivals.shape[0], look, (jnp.int32(0),) * count, unroll=8
    )
    head_of = lax.broadcasted_iota(jnp.int32, (heads, D), 0) // group
    for n in range(count):
        away = (found[n] // head_count) ^ blk
        line = (away // members) * head_count + (lax.rem(found[n], head_count) ^ head_at)
        lines = pl.ds(pl.multiple_of(line * PAD_PARTS, PAD_PARTS), PAD_PARTS)
        x = near[0][lines, :]
        for part in range(1, members):
            x = jnp.where(lax.rem(away, members) == part, near[part][lines, :], x)
        x = x.astype(jnp.float32)
        angle = lengths[n].astype(jnp.float32) * frequency[...]
        lane = lax.broadcasted_iota(jnp.int32, angle.shape, 1)
        sine = jnp.sin(angle)
        turned = turn(x, jnp.cos(angle), jnp.where(lane < D // 2, -sine, sine))
        turned = turned.astype(jnp.bfloat16).astype(jnp.float32)
        q = turned[:heads]
        wide = [jnp.where(head_of == kv, q, 0.0) for kv in range(kv_heads)]
        wide = jnp.concatenate(wide, axis=1).astype(jnp.bfloat16)
        new_key = jnp.zeros((heads, D), jnp.float32)
        new_value = jnp.zeros((heads, D), jnp.float32)
        for kv in range(kv_heads):
            key = turned[heads + kv : heads + kv + 1]
            value = x[heads + kv_heads + kv : heads + kv_heads + kv + 1]
            new_key = jnp.where(head_of == kv, key, new_key)
            new_value = jnp.where(head_of == kv, value, new_value)
        s = lax.dot_general(
            wide, cache[0, n], (((1,), (1,)), ((), ())), preferred_element_type=jnp.float32
        )
        slot = lax.broadcasted_iota(jnp.int32, (heads, slots), 1)
        s = jnp.where(slot < lengths[n], s, HIDDEN)
        own_s = jnp.sum(q * new_key, axis=1, keepdims=True)
        top = jnp.maximum(jnp.max(s, axis=1, keepdims=True), own_s)
        w = jnp.exp2((s - top) * LOG2_SCALE)
        own_w = jnp.exp2((own_s - top) * LOG2_SCALE)
        mass = jnp.sum(w, axis=1, keepdims=True) + own_w
        mix = jnp.dot(w.astype(jnp.bfloat16), cache[1, n], preferred_element_type=jnp.float32)
        picked = own_w.astype(jnp.bfloat16).astype(jnp.float32) * new_value
        for kv in range(kv_heads):
            picked = picked + jnp.where(head_of == kv, mix[:, kv * D : (kv + 1) * D], 0.0)
        picked = picked / mass
        for head in range(heads):
            mixed[n : n + 1, head * D : (head + 1) * D] = picked[head : head + 1, :]
    out[...] = mixed[...].astype(out.dtype)


def exchange(block, axis, distance):
    count = lax.axis_size(axis)
    return lax.ppermute(block, axis, [(i, i ^ distance) for i in range(count)])


NEAR = pl.BlockSpec(memory_space=pltpu.VMEM)
FAR = pl.BlockSpec(memory_space=pltpu.MemorySpace.HBM)
def stay(*arrays):
    return [pltpu.with_memory_space_constraint(a, pltpu.MemorySpace.HBM) for a in arrays]


SCALARS = pl.BlockSpec(memory_space=pltpu.SMEM)


def shards(
    long_query,
    long_new_kv,
    sink_kv,
    window,
    long_len,
    long_offset,
    dec_query,
    dec_new_kv,
    dec_cache,
    dec_len,
    arrival_order,
):
    blk_count, head_count = lax.axis_size("blk"), lax.axis_size("head")
    rows, features = long_query.shape
    heads = features // D
    kv_width = long_new_kv.shape[2]
    kv_heads = kv_width // D
    group = heads // kv_heads
    slots = window.shape[1]
    members = SPAN // rows
    own_count = dec_cache.shape[1]

    queries = [long_query] + [exchange(long_query, "blk", part) for part in range(1, members)]

    half = jnp.arange(D, dtype=jnp.int32) % (D // 2)
    frequency = (10000.0 ** (-(half.astype(jnp.float32) * 2.0 / D))).reshape(1, D)

    def call(kernel, out_shape, operands, specs, scratch):
        return pl.pallas_call(
            kernel,
            in_specs=specs,
            out_specs=jax.tree.map(lambda _: NEAR, out_shape),
            out_shape=out_shape,
            scratch_shapes=scratch,
            compiler_params=VMEM,
        )(*operands)

    pieces = call(
        spread_kernel,
        (jax.ShapeDtypeStruct((PAD_PARTS, D), jnp.bfloat16),) * head_count,
        stay(dec_query, dec_new_kv),
        [FAR, FAR],
        [
            pltpu.VMEM(dec_query.shape, jnp.bfloat16),
            pltpu.VMEM(dec_new_kv.shape, jnp.bfloat16),
            pltpu.SemaphoreType.DMA((2,)),
        ],
    )
    arrived = jnp.concatenate(
        [exchange(piece, "head", r) if r else piece for r, piece in enumerate(pieces)], axis=0
    )
    distance = members
    while distance < blk_count:
        arrived = jnp.concatenate([arrived, exchange(arrived, "blk", distance)], axis=0)
        distance *= 2
    near = [arrived] + [exchange(arrived, "blk", part) for part in range(1, members)]

    total = slots + rows + D
    shared = call(
        prepare_kernel,
        (
            jax.ShapeDtypeStruct((total, kv_width), jnp.bfloat16),
            jax.ShapeDtypeStruct((kv_width, total), jnp.bfloat16),
            jax.ShapeDtypeStruct((members, rows, D), jnp.float32),
            jax.ShapeDtypeStruct((members, rows, D), jnp.float32),
            jax.ShapeDtypeStruct((members, total, rows), jnp.float32),
        ),
        (*stay(long_len, long_offset, long_new_kv, sink_kv, window), frequency),
        [FAR] * 5 + [NEAR],
        [
            pltpu.SMEM(long_len.shape, jnp.int32),
            pltpu.SMEM(long_offset.shape, jnp.int32),
            pltpu.VMEM(long_new_kv.shape, jnp.bfloat16),
            pltpu.VMEM((2, *sink_kv.shape[2:]), jnp.bfloat16),
            pltpu.VMEM(window.shape[1:], jnp.bfloat16),
            pltpu.VMEM((D, kv_width), jnp.float32),
            pltpu.SemaphoreType.DMA((6,)),
        ],
    )

    def attend(part):
        own = part == 0
        if own:
            out = jax.ShapeDtypeStruct((features + heads, rows), jnp.float32)
        else:
            out = jax.ShapeDtypeStruct((features + 4 * heads, rows), jnp.bfloat16)
        return call(
            functools.partial(attend_kernel, part, own),
            out,
            (queries[part], *shared),
            [NEAR] * 6,
            [
                pltpu.VMEM((total, group * rows), jnp.float32),
                pltpu.VMEM((total, group * rows), jnp.bfloat16),
            ],
        )

    mine = attend(0)
    others = [exchange(attend(part), "blk", part) for part in range(1, members)]
    long_out = call(
        combine_kernel,
        jax.ShapeDtypeStruct((rows, features), jnp.bfloat16),
        (mine, *others),
        [NEAR] * (1 + len(others)),
        [],
    )
    dec_out = call(
        decode_kernel,
        jax.ShapeDtypeStruct((own_count, features), jnp.bfloat16),
        (dec_len, arrival_order, *near, dec_cache, frequency),
        [SCALARS, SCALARS] + [NEAR] * (len(near) + 2),
        [
            pltpu.VMEM((own_count, features), jnp.float32),
        ],
    )
    return (long_out, dec_out)


def solution(mesh):
    in_specs = (
        P("blk", "head"),
        P(None, "blk", "head"),
        P(None, None, None, "head"),
        P(None, "blk", "head"),
        P(),
        P(),
        P(("blk", "head"), None),
        P(("blk", "head"), None, None),
        P(None, "blk", None, "head"),
        P("blk"),
        P(),
    )
    out_specs = (P("blk", "head"), P("blk", "head"))
    return jax.shard_map(shards, mesh=mesh, in_specs=in_specs, out_specs=out_specs, check_vma=False)
```

```python
import functools
import math

import jax
import jax.numpy as jnp
from jax import lax
from jax.experimental import pallas as pl
from jax.experimental.pallas import tpu as pltpu
from jax.sharding import PartitionSpec as P

D = 128
W = 4096
SINKS = 4
SPAN = 512
PAD_PARTS = 16
LOG_LINES = 4
HIDDEN = -1e30
LOG2_SCALE = math.log2(math.e) / math.sqrt(D)
VMEM = pltpu.CompilerParams(vmem_limit_bytes=24 * 1024 * 1024)


def turn(x, cosine, sine):
    return x * cosine + pltpu.roll(x, D // 2, 1) * sine


def split_three(x):
    high = x.astype(jnp.bfloat16)
    rest = x - high.astype(jnp.float32)
    middle = rest.astype(jnp.bfloat16)
    low = (rest - middle.astype(jnp.float32)).astype(jnp.bfloat16)
    return high, middle, low


def angle_tables(length, first_step, frequency):
    half = D // 2
    line = lax.broadcasted_iota(jnp.int32, (half, D), 0)
    lane = lax.broadcasted_iota(jnp.int32, (half, D), 1)
    low = lane < half
    position = length + first_step + line + jnp.where(low, 0, half)
    angle = position.astype(jnp.float32) * frequency
    cosine, sine = jnp.cos(angle), jnp.sin(angle)
    cosine_r, sine_r = pltpu.roll(cosine, half, 1), pltpu.roll(sine, half, 1)
    cosines = [jnp.where(low, cosine, cosine_r), jnp.where(low, cosine_r, cosine)]
    sines = [jnp.where(low, -sine, sine_r), jnp.where(low, -sine_r, sine)]
    return jnp.concatenate(cosines, axis=0), jnp.concatenate(sines, axis=0)


def whereabouts(rows):
    members = SPAN // rows
    blk = lax.axis_index("blk")
    return blk // members, lax.rem(blk, members)


def fetch(*pairs):
    copies = [pltpu.make_async_copy(*pair) for pair in pairs]
    for copy in copies:
        copy.start()
    return copies


def spread_kernel(query_far, new_kv_far, *refs):
    pieces, (query, new_kv, arrived) = refs[:-3], refs[-3:]
    for copy in fetch(
        (query_far, query, arrived.at[0]), (new_kv_far, new_kv, arrived.at[1])
    ):
        copy.wait()
    head_at = lax.axis_index("head")
    width = query.shape[1] // len(pieces)
    kv_width = new_kv.shape[2] // len(pieces)

    def lines(ref, size, at):
        found = ref[:, pl.ds(pl.multiple_of(at * size, D), size)].astype(jnp.float32)
        return [
            found[line : line + 1, low : low + D]
            for line in range(found.shape[0])
            for low in range(0, size, D)
        ]

    for distance, piece in enumerate(pieces):
        at = head_at ^ distance
        found = lines(query, width, at) + lines(new_kv.at[0], kv_width, at)
        found.append(jnp.zeros((PAD_PARTS - len(found), D), jnp.float32))
        piece[...] = jnp.concatenate(found, axis=0).astype(piece.dtype)


def prepare_kernel(
    lengths_far,
    offsets_far,
    new_kv_far,
    sinks_far,
    window_far,
    dec_lengths_far,
    frequency,
    keys,
    values_t,
    cosines,
    sines,
    biases,
    dec_tables,
    lengths,
    offsets,
    dec_lengths,
    new_kv,
    sinks,
    values,
    pad,
    arrived,
):
    rows = new_kv.shape[1]
    slots = values.shape[0]
    request, place = whereabouts(rows)
    scalars = fetch(
        (lengths_far, lengths, arrived.at[0]),
        (offsets_far, offsets, arrived.at[1]),
        (dec_lengths_far, dec_lengths, arrived.at[6]),
    )
    arrays = fetch(
        (new_kv_far, new_kv, arrived.at[2]),
        (sinks_far.at[:, request], sinks, arrived.at[3]),
        (window_far.at[1], values, arrived.at[4]),
        (window_far.at[0], keys.at[:slots], arrived.at[5]),
    )
    for copy in scalars:
        copy.wait()
    length, offset = lengths[request], offsets[request]
    filled = jnp.minimum(length - SINKS, W)
    for part in range(cosines.shape[0]):
        first_step = (place ^ part) * rows
        for low in range(0, rows, D):
            lines = slice(low, low + D)
            cosines[part, lines], sines[part, lines] = angle_tables(
                length, first_step + low, frequency[...]
            )
    line = lax.broadcasted_iota(jnp.int32, dec_tables.shape[1:], 0)
    lane = lax.broadcasted_iota(jnp.int32, dec_tables.shape[1:], 1)
    position = jnp.zeros(dec_tables.shape[1:], jnp.int32)
    for n in range(dec_lengths.shape[0]):
        position = jnp.where(line == n, dec_lengths[n], position)
    angle = position.astype(jnp.float32) * frequency[...]
    sine = jnp.sin(angle)
    dec_tables[0] = jnp.cos(angle)
    dec_tables[1] = jnp.where(lane < D // 2, -sine, sine)
    index = lax.broadcasted_iota(jnp.int32, (D, rows), 0)
    step = lax.broadcasted_iota(jnp.int32, (D, rows), 1)
    for low in range(0, slots, D):
        age = (place * slots + low - offset + index) & (W - 1)
        limit = jnp.where(age < filled, age - filled + W, -1)
        for part in range(biases.shape[0]):
            seen = limit > (place ^ part) * rows + step
            biases[part, low : low + D] = jnp.where(seen, 0.0, HIDDEN)
    for low in range(0, rows, D):
        for part in range(biases.shape[0]):
            seen = place * rows + low + index <= (place ^ part) * rows + step
            biases[part, slots + low : slots + low + D] = jnp.where(seen, 0.0, HIDDEN)
    for part in range(biases.shape[0]):
        seen = index < (SINKS if part == 0 else 0)
        biases[part, slots + rows :] = jnp.where(seen, 0.0, HIDDEN)
    for copy in arrays:
        copy.wait()
    for head in range(new_kv.shape[2] // D):
        lanes = slice(head * D, (head + 1) * D)
        key = turn(new_kv[0, :, lanes].astype(jnp.float32), cosines[0], sines[0])
        keys[slots : slots + rows, lanes] = key.astype(jnp.bfloat16)
    for kind in range(2):
        pad[...] = jnp.zeros_like(pad)
        pad[:SINKS, :] = sinks[kind].astype(jnp.float32)
        if kind == 0:
            keys[slots + rows :, :] = pad[...].astype(jnp.bfloat16)
        else:
            values_t[:, slots + rows :] = pad[...].T.astype(jnp.bfloat16)
    values_t[:, :slots] = values[...].T
    values_t[:, slots : slots + rows] = new_kv[1].T


def attend_kernel(part, query, keys, values_t, cosine, sine, bias, *refs):
    own = part == 0
    passengers, (out, scores, weights) = refs[:-3], refs[-3:]
    rows = query.shape[0]
    kv_heads = keys.shape[1] // D
    group = query.shape[1] // D // kv_heads
    total = keys.shape[0] if own else keys.shape[0] - D
    logs = []
    for kv in range(kv_heads):
        lanes = slice(kv * D, (kv + 1) * D)
        turned = []
        for head in range(kv * group, (kv + 1) * group):
            x = query[:, head * D : (head + 1) * D].astype(jnp.float32)
            turned.append(turn(x, cosine[part], sine[part]).astype(jnp.bfloat16))
        block = jnp.concatenate(turned, axis=0)
        top = None
        for low in range(0, total, D):
            chunk = keys[low : low + D, lanes]
            mask = bias[part, low : low + D]
            s = lax.dot_general(
                chunk, block, (((1,), (1,)), ((), ())), preferred_element_type=jnp.float32
            )
            s = s + jnp.concatenate([mask] * group, axis=1)
            scores[kv, low : low + D, :] = s
            peak = jnp.max(s.reshape(D // 8, 8, group * rows), axis=0)
            top = peak if top is None else jnp.maximum(top, peak)
        top = jnp.max(top, axis=0, keepdims=True)
        mass = jnp.zeros((8, group * rows), jnp.float32)
        for low in range(0, total, D):
            w = jnp.exp2((scores[kv, low : low + D, :] - top) * LOG2_SCALE)
            mass = mass + jnp.sum(w.reshape(D // 8, 8, group * rows), axis=0)
            weights[kv, low : low + D, :] = w.astype(jnp.bfloat16)
        mass = jnp.sum(mass, axis=0, keepdims=True)
        mix = jnp.dot(
            values_t[lanes, :total], weights[kv, :total, :], preferred_element_type=jnp.float32
        )
        mix = mix * (1.0 / mass)
        log = top * LOG2_SCALE + jnp.log2(mass)
        for j in range(group):
            head = kv * group + j
            out[head * D : (head + 1) * D, :] = mix[:, j * rows : (j + 1) * rows].astype(out.dtype)
            logs.append(log[:, j * rows : (j + 1) * rows])
    log = jnp.concatenate(logs, axis=0)
    heads = len(logs)
    if own:
        out[heads * D :, :] = log
    else:
        pieces = [p.astype(jnp.float32) for p in split_three(log)]
        pieces.append(jnp.zeros_like(log))
        end = heads * D + LOG_LINES * heads
        out[heads * D : end, :] = jnp.concatenate(pieces, axis=0).astype(out.dtype)
        for block in passengers:
            out[end : end + block.shape[0], :] = block[...]
            end += block.shape[0]


def append_kernel(block, *refs):
    passengers, out = refs[:-1], refs[-1]
    end = block.shape[0]
    for passenger in passengers[::-1]:
        out[end - passenger.shape[0] : end, :] = passenger[...]
        end -= passenger.shape[0]


def combine(own, first, second, third, out):
    heads = out.shape[1] // D
    logs = [own[heads * D :, :]]
    for other in (first, second, third):
        p = other[heads * D : (D + LOG_LINES) * heads, :].astype(jnp.float32)
        logs.append(p[:heads] + p[heads : 2 * heads] + p[2 * heads : 3 * heads])
    top = functools.reduce(jnp.maximum, logs)
    shares = [jnp.exp2(log - top) for log in logs]
    scale = 1.0 / sum(shares)
    shares = [share * scale for share in shares]
    for head in range(heads):
        lines = slice(head * D, (head + 1) * D)
        mix = own[lines, :] * shares[0][head : head + 1, :]
        for other, share in zip((first, second, third), shares[1:]):
            mix = mix + other[lines, :].astype(jnp.float32) * share[head : head + 1, :]
        out[:, lines] = mix.T.astype(out.dtype)


def decode(lengths, arrivals, near, cache, tables, out, mixed):
    count = cache.shape[1]
    slots = cache.shape[2]
    kv_heads = cache.shape[3] // D
    heads = out.shape[1] // D
    group = heads // kv_heads
    blk, head_at = lax.axis_index("blk"), lax.axis_index("head")
    head_count = lax.axis_size("head")
    members = len(near)
    height = near[0].shape[0]

    def look(i, found):
        owner = arrivals[i] - blk * count
        return tuple(jnp.where(owner == n, i, was) for n, was in enumerate(found))

    found = lax.fori_loop(0, arrivals.shape[0], look, (jnp.int32(0),) * count, unroll=8)
    head_of = lax.broadcasted_iota(jnp.int32, (heads, D), 0) // group
    slot = lax.broadcasted_iota(jnp.int32, (heads, slots), 1)
    scores, own_scores, new_values = [], [], []
    for n in range(count):
        away = (found[n] // head_count) ^ blk
        line = (away // members) * head_count + (lax.rem(found[n], head_count) ^ head_at)
        line = line * PAD_PARTS
        x = None
        for part, block in enumerate(near):
            start = pl.multiple_of(block.shape[0] - height + line, PAD_PARTS)
            y = block[pl.ds(start, PAD_PARTS), :]
            x = y if x is None else jnp.where(lax.rem(away, members) == part, y, x)
        x = x.astype(jnp.float32)
        turned = turn(x, tables[0, n : n + 1, :], tables[1, n : n + 1, :])
        turned = turned.astype(jnp.bfloat16).astype(jnp.float32)
        q = turned[:heads]
        wide = [jnp.where(head_of == kv, q, 0.0) for kv in range(kv_heads)]
        wide = jnp.concatenate(wide, axis=1).astype(jnp.bfloat16)
        new_key = jnp.zeros((heads, D), jnp.float32)
        new_value = jnp.zeros((heads, D), jnp.float32)
        for kv in range(kv_heads):
            key = turned[heads + kv : heads + kv + 1]
            value = x[heads + kv_heads + kv : heads + kv_heads + kv + 1]
            new_key = jnp.where(head_of == kv, key, new_key)
            new_value = jnp.where(head_of == kv, value, new_value)
        s = lax.dot_general(
            wide, cache[0, n], (((1,), (1,)), ((), ())), preferred_element_type=jnp.float32
        )
        scores.append(jnp.where(slot < lengths[n], s, HIDDEN))
        own_scores.append(q * new_key)
        new_values.append(new_value)
    s = jnp.concatenate(scores, axis=0)
    own_s = jnp.sum(jnp.concatenate(own_scores, axis=0), axis=1, keepdims=True)
    top = jnp.maximum(jnp.max(s, axis=1, keepdims=True), own_s)
    w = jnp.exp2((s - top) * LOG2_SCALE)
    own_w = jnp.exp2((own_s - top) * LOG2_SCALE)
    scale = 1.0 / (jnp.sum(w, axis=1, keepdims=True) + own_w)
    own_w = own_w.astype(jnp.bfloat16).astype(jnp.float32)
    for n in range(count):
        lines = slice(n * heads, (n + 1) * heads)
        mix = jnp.dot(
            w[lines].astype(jnp.bfloat16), cache[1, n], preferred_element_type=jnp.float32
        )
        picked = own_w[lines] * new_values[n]
        for kv in range(kv_heads):
            picked = picked + jnp.where(head_of == kv, mix[:, kv * D : (kv + 1) * D], 0.0)
        picked = picked * scale[lines]
        for head in range(heads):
            mixed[n : n + 1, head * D : (head + 1) * D] = picked[head : head + 1, :]
    out[...] = mixed[...].astype(out.dtype)


def finish_kernel(
    lengths, arrivals, own, first, second, third, *refs
):
    rows, (cache, tables, long_out, dec_out, mixed, held) = refs[:-6], refs[-6:]
    low = 0
    for block in rows:
        held[low : low + block.shape[0], :] = block[...]
        low += block.shape[0]
    decode(lengths, arrivals, (held, first, second, third), cache, tables, dec_out, mixed)
    combine(own, first, second, third, long_out)


def after(block, *others):
    return lax.optimization_barrier((block, *others))[0]


def exchange(block, axis, distance):
    count = lax.axis_size(axis)
    return lax.ppermute(block, axis, [(i, i ^ distance) for i in range(count)])


NEAR = pl.BlockSpec(memory_space=pltpu.VMEM)
FAR = pl.BlockSpec(memory_space=pltpu.MemorySpace.HBM)
def stay(*arrays):
    return [pltpu.with_memory_space_constraint(a, pltpu.MemorySpace.HBM) for a in arrays]


SCALARS = pl.BlockSpec(memory_space=pltpu.SMEM)


def shards(
    long_query,
    long_new_kv,
    sink_kv,
    window,
    long_len,
    long_offset,
    dec_query,
    dec_new_kv,
    dec_cache,
    dec_len,
    arrival_order,
):
    blk_count, head_count = lax.axis_size("blk"), lax.axis_size("head")
    rows, features = long_query.shape
    heads = features // D
    kv_width = long_new_kv.shape[2]
    kv_heads = kv_width // D
    group = heads // kv_heads
    slots = window.shape[1]
    members = SPAN // rows
    own_count = dec_cache.shape[1]

    queries = {part: exchange(long_query, "blk", part) for part in range(1, members)}

    half = jnp.arange(D, dtype=jnp.int32) % (D // 2)
    frequency = (10000.0 ** (-(half.astype(jnp.float32) * 2.0 / D))).reshape(1, D)

    def call(kernel, out_shape, operands, specs, scratch, aliases={}):
        return pl.pallas_call(
            kernel,
            in_specs=specs,
            out_specs=jax.tree.map(lambda _: NEAR, out_shape),
            out_shape=out_shape,
            scratch_shapes=scratch,
            input_output_aliases=aliases,
            compiler_params=VMEM,
        )(*operands)

    pieces = call(
        spread_kernel,
        (jax.ShapeDtypeStruct((PAD_PARTS, D), jnp.bfloat16),) * head_count,
        stay(dec_query, dec_new_kv),
        [FAR, FAR],
        [
            pltpu.VMEM(dec_query.shape, jnp.bfloat16),
            pltpu.VMEM(dec_new_kv.shape, jnp.bfloat16),
            pltpu.SemaphoreType.DMA((2,)),
        ],
    )
    arrived = jnp.concatenate(
        [exchange(piece, "head", r) if r else piece for r, piece in enumerate(pieces)], axis=0
    )
    total = slots + rows + D
    shared = call(
        prepare_kernel,
        (
            jax.ShapeDtypeStruct((total, kv_width), jnp.bfloat16),
            jax.ShapeDtypeStruct((kv_width, total), jnp.bfloat16),
            jax.ShapeDtypeStruct((members, rows, D), jnp.float32),
            jax.ShapeDtypeStruct((members, rows, D), jnp.float32),
            jax.ShapeDtypeStruct((members, total, rows), jnp.float32),
            jax.ShapeDtypeStruct((2, -(-own_count // 8) * 8, D), jnp.float32),
        ),
        (*stay(long_len, long_offset, long_new_kv, sink_kv, window, dec_len), frequency),
        [FAR] * 6 + [NEAR],
        [
            pltpu.SMEM(long_len.shape, jnp.int32),
            pltpu.SMEM(long_offset.shape, jnp.int32),
            pltpu.SMEM(dec_len.shape, jnp.int32),
            pltpu.VMEM(long_new_kv.shape, jnp.bfloat16),
            pltpu.VMEM((2, *sink_kv.shape[2:]), jnp.bfloat16),
            pltpu.VMEM(window.shape[1:], jnp.bfloat16),
            pltpu.VMEM((D, kv_width), jnp.float32),
            pltpu.SemaphoreType.DMA((7,)),
        ],
    )

    def attend(part, query, spare, *passenger):
        if part == 0:
            out = jax.ShapeDtypeStruct((features + heads, rows), jnp.float32)
        else:
            lines = features + LOG_LINES * heads + spare
            lines += sum(p.shape[0] for p in passenger)
            out = jax.ShapeDtypeStruct((lines, rows), jnp.bfloat16)
        return call(
            functools.partial(attend_kernel, part),
            out,
            (query, *shared[:5], *passenger),
            [NEAR] * (6 + len(passenger)),
            [
                pltpu.VMEM((kv_heads, total, group * rows), jnp.float32),
                pltpu.VMEM((kv_heads, total, group * rows), jnp.bfloat16),
            ],
        )

    arrived = after(arrived, shared[0])
    blocks = [arrived]
    while len(blocks) * arrived.shape[0] * members < arrival_order.shape[0] * PAD_PARTS:
        full = blocks[0] if len(blocks) == 1 else jnp.concatenate(blocks, axis=0)
        blocks = [full, exchange(full, "blk", members * full.shape[0] // arrived.shape[0])]
    spare = sum(block.shape[0] for block in blocks)
    mine = attend(0, long_query, 0)
    backs = {}
    for part in range(1, members):
        if part == members - 1:
            mix = attend(part, queries[part], spare)
            mix = call(
                append_kernel,
                jax.ShapeDtypeStruct(mix.shape, mix.dtype),
                (mix, *blocks),
                [NEAR] * (1 + len(blocks)),
                [],
                {0: 0},
            )
        else:
            mix = attend(part, queries[part], 0, *blocks)
        backs[part] = exchange(mix, "blk", part)
    first_back, second_back, third_back = [backs[part] for part in range(1, members)]
    return call(
        finish_kernel,
        (
            jax.ShapeDtypeStruct((rows, features), jnp.bfloat16),
            jax.ShapeDtypeStruct((own_count, features), jnp.bfloat16),
        ),
        (
            dec_len, arrival_order, mine, first_back, second_back, third_back,
            *blocks, dec_cache, shared[5],
        ),
        [SCALARS, SCALARS] + [NEAR] * (6 + len(blocks)),
        [
            pltpu.VMEM((own_count, features), jnp.float32),
            pltpu.VMEM((spare, D), jnp.bfloat16),
        ],
    )


def solution(mesh):
    in_specs = (
        P("blk", "head"),
        P(None, "blk", "head"),
        P(None, None, None, "head"),
        P(None, "blk", "head"),
        P(),
        P(),
        P(("blk", "head"), None),
        P(("blk", "head"), None, None),
        P(None, "blk", None, "head"),
        P("blk"),
        P(),
    )
    out_specs = (P("blk", "head"), P("blk", "head"))
    return jax.shard_map(shards, mesh=mesh, in_specs=in_specs, out_specs=out_specs, check_vma=False)
```

```python
import functools
import math

import jax
import jax.numpy as jnp
from jax import lax
from jax.experimental import pallas as pl
from jax.experimental.pallas import tpu as pltpu
from jax.sharding import PartitionSpec as P

D = 128
W = 4096
SINKS = 4
SPAN = 512
PAD_PARTS = 16
LOG_LINES = 4
HIDDEN = -1e30
LOG2_SCALE = math.log2(math.e) / math.sqrt(D)
VMEM = pltpu.CompilerParams(vmem_limit_bytes=24 * 1024 * 1024)


def turn(x, cosine, sine):
    return x * cosine + pltpu.roll(x, D // 2, 1) * sine


def split_three(x):
    high = x.astype(jnp.bfloat16)
    rest = x - high.astype(jnp.float32)
    middle = rest.astype(jnp.bfloat16)
    low = (rest - middle.astype(jnp.float32)).astype(jnp.bfloat16)
    return high, middle, low


def angle_tables(length, first_step, frequency):
    half = D // 2
    line = lax.broadcasted_iota(jnp.int32, (half, D), 0)
    lane = lax.broadcasted_iota(jnp.int32, (half, D), 1)
    low = lane < half
    position = length + first_step + line + jnp.where(low, 0, half)
    angle = position.astype(jnp.float32) * frequency
    cosine, sine = jnp.cos(angle), jnp.sin(angle)
    cosine_r, sine_r = pltpu.roll(cosine, half, 1), pltpu.roll(sine, half, 1)
    cosines = [jnp.where(low, cosine, cosine_r), jnp.where(low, cosine_r, cosine)]
    sines = [jnp.where(low, -sine, sine_r), jnp.where(low, -sine_r, sine)]
    return jnp.concatenate(cosines, axis=0), jnp.concatenate(sines, axis=0)


def whereabouts(rows):
    members = SPAN // rows
    blk = lax.axis_index("blk")
    return blk // members, lax.rem(blk, members)


def fetch(*pairs):
    copies = [pltpu.make_async_copy(*pair) for pair in pairs]
    for copy in copies:
        copy.start()
    return copies


def spread_kernel(query_far, new_kv_far, *refs):
    pieces, (query, new_kv, arrived) = refs[:-3], refs[-3:]
    for copy in fetch(
        (query_far, query, arrived.at[0]), (new_kv_far, new_kv, arrived.at[1])
    ):
        copy.wait()
    head_at = lax.axis_index("head")
    width = query.shape[1] // len(pieces)
    kv_width = new_kv.shape[2] // len(pieces)

    def lines(ref, size, at):
        found = ref[:, pl.ds(pl.multiple_of(at * size, D), size)].astype(jnp.float32)
        return [
            found[line : line + 1, low : low + D]
            for line in range(found.shape[0])
            for low in range(0, size, D)
        ]

    for distance, piece in enumerate(pieces):
        at = head_at ^ distance
        found = lines(query, width, at) + lines(new_kv.at[0], kv_width, at)
        found.append(jnp.zeros((PAD_PARTS - len(found), D), jnp.float32))
        piece[...] = jnp.concatenate(found, axis=0).astype(piece.dtype)


def prepare_kernel(
    lengths_far,
    offsets_far,
    new_kv_far,
    sinks_far,
    window_far,
    dec_lengths_far,
    frequency,
    keys,
    values_t,
    cosines,
    sines,
    biases,
    dec_tables,
    lengths,
    offsets,
    dec_lengths,
    new_kv,
    sinks,
    values,
    pad,
    arrived,
):
    rows = new_kv.shape[1]
    slots = values.shape[0]
    request, place = whereabouts(rows)
    scalars = fetch(
        (lengths_far, lengths, arrived.at[0]),
        (offsets_far, offsets, arrived.at[1]),
        (dec_lengths_far, dec_lengths, arrived.at[6]),
    )
    arrays = fetch(
        (new_kv_far, new_kv, arrived.at[2]),
        (sinks_far.at[:, request], sinks, arrived.at[3]),
        (window_far.at[1], values, arrived.at[4]),
        (window_far.at[0], keys.at[:slots], arrived.at[5]),
    )
    for copy in scalars:
        copy.wait()
    length, offset = lengths[request], offsets[request]
    filled = jnp.minimum(length - SINKS, W)
    for part in range(cosines.shape[0]):
        first_step = (place ^ part) * rows
        for low in range(0, rows, D):
            lines = slice(low, low + D)
            cosines[part, lines], sines[part, lines] = angle_tables(
                length, first_step + low, frequency[...]
            )
    line = lax.broadcasted_iota(jnp.int32, dec_tables.shape[1:], 0)
    lane = lax.broadcasted_iota(jnp.int32, dec_tables.shape[1:], 1)
    position = jnp.zeros(dec_tables.shape[1:], jnp.int32)
    for n in range(dec_lengths.shape[0]):
        position = jnp.where(line == n, dec_lengths[n], position)
    angle = position.astype(jnp.float32) * frequency[...]
    sine = jnp.sin(angle)
    dec_tables[0] = jnp.cos(angle)
    dec_tables[1] = jnp.where(lane < D // 2, -sine, sine)
    index = lax.broadcasted_iota(jnp.int32, (D, rows), 0)
    step = lax.broadcasted_iota(jnp.int32, (D, rows), 1)
    for low in range(0, slots, D):
        age = (place * slots + low - offset + index) & (W - 1)
        limit = jnp.where(age < filled, age - filled + W, -1)
        for part in range(biases.shape[0]):
            seen = limit > (place ^ part) * rows + step
            biases[part, low : low + D] = jnp.where(seen, 0.0, HIDDEN)
    for low in range(0, rows, D):
        for part in range(biases.shape[0]):
            seen = place * rows + low + index <= (place ^ part) * rows + step
            biases[part, slots + low : slots + low + D] = jnp.where(seen, 0.0, HIDDEN)
    for part in range(biases.shape[0]):
        seen = index < (SINKS if part == 0 else 0)
        biases[part, slots + rows :] = jnp.where(seen, 0.0, HIDDEN)
    for copy in arrays:
        copy.wait()
    for head in range(new_kv.shape[2] // D):
        lanes = slice(head * D, (head + 1) * D)
        key = turn(new_kv[0, :, lanes].astype(jnp.float32), cosines[0], sines[0])
        keys[slots : slots + rows, lanes] = key.astype(jnp.bfloat16)
    for kind in range(2):
        pad[...] = jnp.zeros_like(pad)
        pad[:SINKS, :] = sinks[kind].astype(jnp.float32)
        if kind == 0:
            keys[slots + rows :, :] = pad[...].astype(jnp.bfloat16)
        else:
            values_t[:, slots + rows :] = pad[...].T.astype(jnp.bfloat16)
    values_t[:, :slots] = values[...].T
    values_t[:, slots : slots + rows] = new_kv[1].T


def attend_kernel(part, query, keys, values_t, cosine, sine, bias, *refs):
    own = part == 0
    passengers, (out, scores, weights) = refs[:-3], refs[-3:]
    rows = query.shape[0]
    kv_heads = keys.shape[1] // D
    group = query.shape[1] // D // kv_heads
    total = keys.shape[0] if own else keys.shape[0] - D
    logs = []
    for kv in range(kv_heads):
        lanes = slice(kv * D, (kv + 1) * D)
        turned = []
        for head in range(kv * group, (kv + 1) * group):
            x = query[:, head * D : (head + 1) * D].astype(jnp.float32)
            turned.append(turn(x, cosine[part], sine[part]).astype(jnp.bfloat16))
        block = jnp.concatenate(turned, axis=0)
        top = None
        for low in range(0, total, D):
            chunk = keys[low : low + D, lanes]
            mask = bias[part, low : low + D]
            s = lax.dot_general(
                chunk, block, (((1,), (1,)), ((), ())), preferred_element_type=jnp.float32
            )
            s = s + jnp.concatenate([mask] * group, axis=1)
            scores[kv, low : low + D, :] = s
            peak = jnp.max(s.reshape(D // 8, 8, group * rows), axis=0)
            top = peak if top is None else jnp.maximum(top, peak)
        top = jnp.max(top, axis=0, keepdims=True)
        mass = jnp.zeros((8, group * rows), jnp.float32)
        for low in range(0, total, D):
            w = jnp.exp2((scores[kv, low : low + D, :] - top) * LOG2_SCALE)
            mass = mass + jnp.sum(w.reshape(D // 8, 8, group * rows), axis=0)
            weights[kv, low : low + D, :] = w.astype(jnp.bfloat16)
        mass = jnp.sum(mass, axis=0, keepdims=True)
        mix = jnp.dot(
            values_t[lanes, :total], weights[kv, :total, :], preferred_element_type=jnp.float32
        )
        mix = mix * (1.0 / mass)
        log = top * LOG2_SCALE + jnp.log2(mass)
        for j in range(group):
            head = kv * group + j
            out[head * D : (head + 1) * D, :] = mix[:, j * rows : (j + 1) * rows].astype(out.dtype)
            logs.append(log[:, j * rows : (j + 1) * rows])
    log = jnp.concatenate(logs, axis=0)
    heads = len(logs)
    if own:
        out[heads * D :, :] = log
    else:
        pieces = [p.astype(jnp.float32) for p in split_three(log)]
        pieces.append(jnp.zeros_like(log))
        end = heads * D + LOG_LINES * heads
        out[heads * D : end, :] = jnp.concatenate(pieces, axis=0).astype(out.dtype)
        for block in passengers:
            out[end : end + block.shape[0], :] = block[...]
            end += block.shape[0]


def append_kernel(block, *refs):
    passengers, out = refs[:-1], refs[-1]
    end = block.shape[0]
    for passenger in passengers[::-1]:
        out[end - passenger.shape[0] : end, :] = passenger[...]
        end -= passenger.shape[0]


def combine(own, first, second, third, out):
    heads = out.shape[1] // D
    logs = [own[heads * D :, :]]
    for other in (first, second, third):
        p = other[heads * D : (D + LOG_LINES) * heads, :].astype(jnp.float32)
        logs.append(p[:heads] + p[heads : 2 * heads] + p[2 * heads : 3 * heads])
    top = functools.reduce(jnp.maximum, logs)
    shares = [jnp.exp2(log - top) for log in logs]
    scale = 1.0 / sum(shares)
    shares = [share * scale for share in shares]
    for head in range(heads):
        lines = slice(head * D, (head + 1) * D)
        mix = own[lines, :] * shares[0][head : head + 1, :]
        for other, share in zip((first, second, third), shares[1:]):
            mix = mix + other[lines, :].astype(jnp.float32) * share[head : head + 1, :]
        out[:, lines] = mix.T.astype(out.dtype)


def decode(lengths, arrivals, near, cache, tables, out, mixed):
    count = cache.shape[1]
    slots = cache.shape[2]
    kv_heads = cache.shape[3] // D
    heads = out.shape[1] // D
    group = heads // kv_heads
    blk, head_at = lax.axis_index("blk"), lax.axis_index("head")
    head_count = lax.axis_size("head")
    members = len(near)
    height = near[0].shape[0]

    def look(i, found):
        owner = arrivals[i] - blk * count
        return tuple(jnp.where(owner == n, i, was) for n, was in enumerate(found))

    found = lax.fori_loop(0, arrivals.shape[0], look, (jnp.int32(0),) * count, unroll=8)
    head_of = lax.broadcasted_iota(jnp.int32, (heads, D), 0) // group
    slot = lax.broadcasted_iota(jnp.int32, (heads, slots), 1)
    scores, own_scores, new_values = [], [], []
    for n in range(count):
        away = (found[n] // head_count) ^ blk
        line = (away // members) * head_count + (lax.rem(found[n], head_count) ^ head_at)
        line = line * PAD_PARTS
        x = None
        for part, block in enumerate(near):
            start = pl.multiple_of(block.shape[0] - height + line, PAD_PARTS)
            y = block[pl.ds(start, PAD_PARTS), :]
            x = y if x is None else jnp.where(lax.rem(away, members) == part, y, x)
        x = x.astype(jnp.float32)
        turned = turn(x, tables[0, n : n + 1, :], tables[1, n : n + 1, :])
        turned = turned.astype(jnp.bfloat16).astype(jnp.float32)
        q = turned[:heads]
        wide = [jnp.where(head_of == kv, q, 0.0) for kv in range(kv_heads)]
        wide = jnp.concatenate(wide, axis=1).astype(jnp.bfloat16)
        new_key = jnp.zeros((heads, D), jnp.float32)
        new_value = jnp.zeros((heads, D), jnp.float32)
        for kv in range(kv_heads):
            key = turned[heads + kv : heads + kv + 1]
            value = x[heads + kv_heads + kv : heads + kv_heads + kv + 1]
            new_key = jnp.where(head_of == kv, key, new_key)
            new_value = jnp.where(head_of == kv, value, new_value)
        s = lax.dot_general(
            wide, cache[0, n], (((1,), (1,)), ((), ())), preferred_element_type=jnp.float32
        )
        scores.append(jnp.where(slot < lengths[n], s, HIDDEN))
        own_scores.append(q * new_key)
        new_values.append(new_value)
    s = jnp.concatenate(scores, axis=0)
    own_s = jnp.sum(jnp.concatenate(own_scores, axis=0), axis=1, keepdims=True)
    top = jnp.maximum(jnp.max(s, axis=1, keepdims=True), own_s)
    w = jnp.exp2((s - top) * LOG2_SCALE)
    own_w = jnp.exp2((own_s - top) * LOG2_SCALE)
    scale = 1.0 / (jnp.sum(w, axis=1, keepdims=True) + own_w)
    own_w = own_w.astype(jnp.bfloat16).astype(jnp.float32)
    for n in range(count):
        lines = slice(n * heads, (n + 1) * heads)
        mix = jnp.dot(
            w[lines].astype(jnp.bfloat16), cache[1, n], preferred_element_type=jnp.float32
        )
        picked = own_w[lines] * new_values[n]
        for kv in range(kv_heads):
            picked = picked + jnp.where(head_of == kv, mix[:, kv * D : (kv + 1) * D], 0.0)
        picked = picked * scale[lines]
        for head in range(heads):
            mixed[n : n + 1, head * D : (head + 1) * D] = picked[head : head + 1, :]
    out[...] = mixed[...].astype(out.dtype)


def finish_kernel(
    lengths, arrivals, own, first, second, third, *refs
):
    rows, (cache, tables, long_out, dec_out, mixed, held) = refs[:-6], refs[-6:]
    low = 0
    for block in rows:
        held[low : low + block.shape[0], :] = block[...]
        low += block.shape[0]
    decode(lengths, arrivals, (held, first, second, third), cache, tables, dec_out, mixed)
    combine(own, first, second, third, long_out)


def after(block, *others):
    return lax.optimization_barrier((block, *others))[0]


def exchange(block, axis, distance):
    count = lax.axis_size(axis)
    return lax.ppermute(block, axis, [(i, i ^ distance) for i in range(count)])


NEAR = pl.BlockSpec(memory_space=pltpu.VMEM)
FAR = pl.BlockSpec(memory_space=pltpu.MemorySpace.HBM)
def stay(*arrays):
    return [pltpu.with_memory_space_constraint(a, pltpu.MemorySpace.HBM) for a in arrays]


SCALARS = pl.BlockSpec(memory_space=pltpu.SMEM)


def shards(
    long_query,
    long_new_kv,
    sink_kv,
    window,
    long_len,
    long_offset,
    dec_query,
    dec_new_kv,
    dec_cache,
    dec_len,
    arrival_order,
):
    blk_count, head_count = lax.axis_size("blk"), lax.axis_size("head")
    rows, features = long_query.shape
    heads = features // D
    kv_width = long_new_kv.shape[2]
    kv_heads = kv_width // D
    group = heads // kv_heads
    slots = window.shape[1]
    members = SPAN // rows
    own_count = dec_cache.shape[1]

    queries = {part: exchange(long_query, "blk", part) for part in range(1, members)}

    half = jnp.arange(D, dtype=jnp.int32) % (D // 2)
    frequency = (10000.0 ** (-(half.astype(jnp.float32) * 2.0 / D))).reshape(1, D)

    def call(kernel, out_shape, operands, specs, scratch, aliases={}):
        return pl.pallas_call(
            kernel,
            in_specs=specs,
            out_specs=jax.tree.map(lambda _: NEAR, out_shape),
            out_shape=out_shape,
            scratch_shapes=scratch,
            input_output_aliases=aliases,
            compiler_params=VMEM,
        )(*operands)

    pieces = call(
        spread_kernel,
        (jax.ShapeDtypeStruct((PAD_PARTS, D), jnp.bfloat16),) * head_count,
        stay(dec_query, dec_new_kv),
        [FAR, FAR],
        [
            pltpu.VMEM(dec_query.shape, jnp.bfloat16),
            pltpu.VMEM(dec_new_kv.shape, jnp.bfloat16),
            pltpu.SemaphoreType.DMA((2,)),
        ],
    )
    arrived = jnp.concatenate(
        [exchange(piece, "head", r) if r else piece for r, piece in enumerate(pieces)], axis=0
    )
    total = slots + rows + D
    shared = call(
        prepare_kernel,
        (
            jax.ShapeDtypeStruct((total, kv_width), jnp.bfloat16),
            jax.ShapeDtypeStruct((kv_width, total), jnp.bfloat16),
            jax.ShapeDtypeStruct((members, rows, D), jnp.float32),
            jax.ShapeDtypeStruct((members, rows, D), jnp.float32),
            jax.ShapeDtypeStruct((members, total, rows), jnp.float32),
            jax.ShapeDtypeStruct((2, -(-own_count // 8) * 8, D), jnp.float32),
        ),
        (*stay(long_len, long_offset, long_new_kv, sink_kv, window, dec_len), frequency),
        [FAR] * 6 + [NEAR],
        [
            pltpu.SMEM(long_len.shape, jnp.int32),
            pltpu.SMEM(long_offset.shape, jnp.int32),
            pltpu.SMEM(dec_len.shape, jnp.int32),
            pltpu.VMEM(long_new_kv.shape, jnp.bfloat16),
            pltpu.VMEM((2, *sink_kv.shape[2:]), jnp.bfloat16),
            pltpu.VMEM(window.shape[1:], jnp.bfloat16),
            pltpu.VMEM((D, kv_width), jnp.float32),
            pltpu.SemaphoreType.DMA((7,)),
        ],
    )

    def attend(part, query, spare, *passenger):
        if part == 0:
            out = jax.ShapeDtypeStruct((features + heads, rows), jnp.float32)
        else:
            lines = features + LOG_LINES * heads + spare
            lines += sum(p.shape[0] for p in passenger)
            out = jax.ShapeDtypeStruct((lines, rows), jnp.bfloat16)
        return call(
            functools.partial(attend_kernel, part),
            out,
            (query, *shared[:5], *passenger),
            [NEAR] * (6 + len(passenger)),
            [
                pltpu.VMEM((kv_heads, total, group * rows), jnp.float32),
                pltpu.VMEM((kv_heads, total, group * rows), jnp.bfloat16),
            ],
        )

    arrived = after(arrived, shared[0])
    blocks, distance = [arrived], members
    while distance < blk_count:
        full = blocks[0] if len(blocks) == 1 else jnp.concatenate(blocks, axis=0)
        blocks = [full, exchange(full, "blk", distance)]
        distance *= 2
    spare = sum(block.shape[0] for block in blocks)
    mine = attend(0, long_query, 0)
    backs = {}
    for part in range(1, members):
        if part == members - 1:
            mix = attend(part, queries[part], spare)
            mix = call(
                append_kernel,
                jax.ShapeDtypeStruct(mix.shape, mix.dtype),
                (mix, *blocks),
                [NEAR] * (1 + len(blocks)),
                [],
                {0: 0},
            )
        else:
            mix = attend(part, queries[part], 0, *blocks)
        backs[part] = exchange(mix, "blk", part)
    first_back, second_back, third_back = [backs[part] for part in range(1, members)]
    return call(
        finish_kernel,
        (
            jax.ShapeDtypeStruct((rows, features), jnp.bfloat16),
            jax.ShapeDtypeStruct((own_count, features), jnp.bfloat16),
        ),
        (
            dec_len, arrival_order, mine, first_back, second_back, third_back,
            *blocks, dec_cache, shared[5],
        ),
        [SCALARS, SCALARS] + [NEAR] * (6 + len(blocks)),
        [
            pltpu.VMEM((own_count, features), jnp.float32),
            pltpu.VMEM((spare, D), jnp.bfloat16),
        ],
    )


def solution(mesh):
    in_specs = (
        P("blk", "head"),
        P(None, "blk", "head"),
        P(None, None, None, "head"),
        P(None, "blk", "head"),
        P(),
        P(),
        P(("blk", "head"), None),
        P(("blk", "head"), None, None),
        P(None, "blk", None, "head"),
        P("blk"),
        P(),
    )
    out_specs = (P("blk", "head"), P("blk", "head"))
    return jax.shard_map(shards, mesh=mesh, in_specs=in_specs, out_specs=out_specs, check_vma=False)
```

```python
import functools
import math

import jax
import jax.numpy as jnp
from jax import lax
from jax.experimental import pallas as pl
from jax.experimental.pallas import tpu as pltpu
from jax.sharding import PartitionSpec as P

D = 128
W = 4096
SINKS = 4
SPAN = 512
PAD_PARTS = 16
LOG_LINES = 4
HIDDEN = -1e30
LOG2_SCALE = math.log2(math.e) / math.sqrt(D)
VMEM = pltpu.CompilerParams(vmem_limit_bytes=24 * 1024 * 1024)


def turn(x, cosine, sine):
    return x * cosine + pltpu.roll(x, D // 2, 1) * sine


def split_three(x):
    high = x.astype(jnp.bfloat16)
    rest = x - high.astype(jnp.float32)
    middle = rest.astype(jnp.bfloat16)
    low = (rest - middle.astype(jnp.float32)).astype(jnp.bfloat16)
    return high, middle, low


def angle_tables(length, first_step, frequency):
    half = D // 2
    line = lax.broadcasted_iota(jnp.int32, (half, D), 0)
    lane = lax.broadcasted_iota(jnp.int32, (half, D), 1)
    low = lane < half
    position = length + first_step + line + jnp.where(low, 0, half)
    angle = position.astype(jnp.float32) * frequency
    cosine, sine = jnp.cos(angle), jnp.sin(angle)
    cosine_r, sine_r = pltpu.roll(cosine, half, 1), pltpu.roll(sine, half, 1)
    cosines = [jnp.where(low, cosine, cosine_r), jnp.where(low, cosine_r, cosine)]
    sines = [jnp.where(low, -sine, sine_r), jnp.where(low, -sine_r, sine)]
    return jnp.concatenate(cosines, axis=0), jnp.concatenate(sines, axis=0)


def whereabouts(rows):
    members = SPAN // rows
    blk = lax.axis_index("blk")
    return blk // members, lax.rem(blk, members)


def fetch(*pairs):
    copies = [pltpu.make_async_copy(*pair) for pair in pairs]
    for copy in copies:
        copy.start()
    return copies


def spread_kernel(query_far, new_kv_far, *refs):
    pieces, (query, new_kv, arrived) = refs[:-3], refs[-3:]
    for copy in fetch(
        (query_far, query, arrived.at[0]), (new_kv_far, new_kv, arrived.at[1])
    ):
        copy.wait()
    head_at = lax.axis_index("head")
    width = query.shape[1] // len(pieces)
    kv_width = new_kv.shape[2] // len(pieces)

    def lines(ref, size, at):
        found = ref[:, pl.ds(pl.multiple_of(at * size, D), size)].astype(jnp.float32)
        return [
            found[line : line + 1, low : low + D]
            for line in range(found.shape[0])
            for low in range(0, size, D)
        ]

    for distance, piece in enumerate(pieces):
        at = head_at ^ distance
        found = lines(query, width, at) + lines(new_kv.at[0], kv_width, at)
        found.append(jnp.zeros((PAD_PARTS - len(found), D), jnp.float32))
        piece[...] = jnp.concatenate(found, axis=0).astype(piece.dtype)


def prepare_kernel(
    lengths_far,
    offsets_far,
    new_kv_far,
    sinks_far,
    window_far,
    dec_lengths_far,
    frequency,
    keys,
    values_t,
    cosines,
    sines,
    biases,
    dec_tables,
    lengths,
    offsets,
    dec_lengths,
    new_kv,
    sinks,
    values,
    pad,
    arrived,
):
    rows = new_kv.shape[1]
    slots = values.shape[0]
    request, place = whereabouts(rows)
    scalars = fetch(
        (lengths_far, lengths, arrived.at[0]),
        (offsets_far, offsets, arrived.at[1]),
        (dec_lengths_far, dec_lengths, arrived.at[6]),
    )
    arrays = fetch(
        (new_kv_far, new_kv, arrived.at[2]),
        (sinks_far.at[:, request], sinks, arrived.at[3]),
        (window_far.at[1], values, arrived.at[4]),
        (window_far.at[0], keys.at[:slots], arrived.at[5]),
    )
    for copy in scalars:
        copy.wait()
    length, offset = lengths[request], offsets[request]
    filled = jnp.minimum(length - SINKS, W)
    for part in range(cosines.shape[0]):
        first_step = (place ^ part) * rows
        for low in range(0, rows, D):
            lines = slice(low, low + D)
            cosines[part, lines], sines[part, lines] = angle_tables(
                length, first_step + low, frequency[...]
            )
    line = lax.broadcasted_iota(jnp.int32, dec_tables.shape[1:], 0)
    lane = lax.broadcasted_iota(jnp.int32, dec_tables.shape[1:], 1)
    position = jnp.zeros(dec_tables.shape[1:], jnp.int32)
    for n in range(dec_lengths.shape[0]):
        position = jnp.where(line == n, dec_lengths[n], position)
    angle = position.astype(jnp.float32) * frequency[...]
    sine = jnp.sin(angle)
    dec_tables[0] = jnp.cos(angle)
    dec_tables[1] = jnp.where(lane < D // 2, -sine, sine)
    index = lax.broadcasted_iota(jnp.int32, (D, rows), 0)
    step = lax.broadcasted_iota(jnp.int32, (D, rows), 1)
    for low in range(0, slots, D):
        age = (place * slots + low - offset + index) & (W - 1)
        limit = jnp.where(age < filled, age - filled + W, -1)
        for part in range(biases.shape[0]):
            seen = limit > (place ^ part) * rows + step
            biases[part, low : low + D] = jnp.where(seen, 0.0, HIDDEN)
    for low in range(0, rows, D):
        for part in range(biases.shape[0]):
            seen = place * rows + low + index <= (place ^ part) * rows + step
            biases[part, slots + low : slots + low + D] = jnp.where(seen, 0.0, HIDDEN)
    for part in range(biases.shape[0]):
        seen = index < (SINKS if part == 0 else 0)
        biases[part, slots + rows :] = jnp.where(seen, 0.0, HIDDEN)
    for copy in arrays:
        copy.wait()
    for head in range(new_kv.shape[2] // D):
        lanes = slice(head * D, (head + 1) * D)
        key = turn(new_kv[0, :, lanes].astype(jnp.float32), cosines[0], sines[0])
        keys[slots : slots + rows, lanes] = key.astype(jnp.bfloat16)
    for kind in range(2):
        pad[...] = jnp.zeros_like(pad)
        pad[:SINKS, :] = sinks[kind].astype(jnp.float32)
        if kind == 0:
            keys[slots + rows :, :] = pad[...].astype(jnp.bfloat16)
        else:
            values_t[:, slots + rows :] = pad[...].T.astype(jnp.bfloat16)
    values_t[:, :slots] = values[...].T
    values_t[:, slots : slots + rows] = new_kv[1].T


def attend_kernel(part, query, keys, values_t, cosine, sine, bias, *refs):
    own = part == 0
    passengers, (out, scores, weights) = refs[:-3], refs[-3:]
    rows = query.shape[0]
    kv_heads = keys.shape[1] // D
    group = query.shape[1] // D // kv_heads
    total = keys.shape[0] if own else keys.shape[0] - D
    share = group
    heads = kv_heads * group
    units = heads // share
    blocks, tops, masses, logs = {}, {}, {}, []

    def score_unit(unit, low):
        kv = unit
        lanes = slice(kv * D, (kv + 1) * D)
        if low == 0:
            turned = []
            for head in range(unit * share, (unit + 1) * share):
                x = query[:, head * D : (head + 1) * D].astype(jnp.float32)
                turned.append(turn(x, cosine[part], sine[part]).astype(jnp.bfloat16))
            blocks[unit] = jnp.concatenate(turned, axis=0)
        s = lax.dot_general(
            keys[low : low + D, lanes],
            blocks[unit],
            (((1,), (1,)), ((), ())),
            preferred_element_type=jnp.float32,
        )
        s = s + jnp.concatenate([bias[part, low : low + D]] * share, axis=1)
        scores[unit, low : low + D, :] = s
        peak = jnp.max(s.reshape(D // 8, 8, share * rows), axis=0)
        tops[unit] = peak if low == 0 else jnp.maximum(tops[unit], peak)

    def weigh_unit(unit, low):
        if low == 0:
            tops[unit] = jnp.max(tops[unit], axis=0, keepdims=True)
        w = jnp.exp2((scores[unit, low : low + D, :] - tops[unit]) * LOG2_SCALE)
        mass = jnp.sum(w.reshape(D // 8, 8, share * rows), axis=0)
        masses[unit] = mass if low == 0 else masses[unit] + mass
        weights[unit, low : low + D, :] = w.astype(jnp.bfloat16)

    def finish_unit(unit):
        kv = unit
        mass = jnp.sum(masses[unit], axis=0, keepdims=True)
        mix = jnp.dot(
            values_t[kv * D : (kv + 1) * D, :total],
            weights[unit, :total, :],
            preferred_element_type=jnp.float32,
        )
        mix = mix * (1.0 / mass)
        log = tops[unit] * LOG2_SCALE + jnp.log2(mass)
        for j in range(share):
            head = unit * share + j
            out[head * D : (head + 1) * D, :] = mix[:, j * rows : (j + 1) * rows].astype(out.dtype)
            logs.append(log[:, j * rows : (j + 1) * rows])

    for step in range(units + 2):
        if step >= 2:
            finish_unit(step - 2)
        for low in range(0, total, D):
            if step < units:
                score_unit(step, low)
            if 1 <= step <= units:
                weigh_unit(step - 1, low)
    log = jnp.concatenate(logs, axis=0)
    if own:
        out[heads * D :, :] = log
    else:
        pieces = [p.astype(jnp.float32) for p in split_three(log)]
        pieces.append(jnp.zeros_like(log))
        end = heads * D + LOG_LINES * heads
        out[heads * D : end, :] = jnp.concatenate(pieces, axis=0).astype(out.dtype)
        for block in passengers:
            out[end : end + block.shape[0], :] = block[...]
            end += block.shape[0]


def append_kernel(block, *refs):
    passengers, out = refs[:-1], refs[-1]
    end = block.shape[0]
    for passenger in passengers[::-1]:
        out[end - passenger.shape[0] : end, :] = passenger[...]
        end -= passenger.shape[0]


def combine(own, first, second, third, out):
    heads = out.shape[1] // D
    logs = [own[heads * D :, :]]
    for other in (first, second, third):
        p = other[heads * D : (D + LOG_LINES) * heads, :].astype(jnp.float32)
        logs.append(p[:heads] + p[heads : 2 * heads] + p[2 * heads : 3 * heads])
    top = functools.reduce(jnp.maximum, logs)
    shares = [jnp.exp2(log - top) for log in logs]
    scale = 1.0 / sum(shares)
    shares = [share * scale for share in shares]
    for head in range(heads):
        lines = slice(head * D, (head + 1) * D)
        mix = own[lines, :] * shares[0][head : head + 1, :]
        for other, share in zip((first, second, third), shares[1:]):
            mix = mix + other[lines, :].astype(jnp.float32) * share[head : head + 1, :]
        out[:, lines] = mix.T.astype(out.dtype)


def decode(lengths, arrivals, near, cache, tables, out, mixed):
    count = cache.shape[1]
    slots = cache.shape[2]
    kv_heads = cache.shape[3] // D
    heads = out.shape[1] // D
    group = heads // kv_heads
    blk, head_at = lax.axis_index("blk"), lax.axis_index("head")
    head_count = lax.axis_size("head")
    members = len(near)
    height = near[0].shape[0]

    def look(i, found):
        owner = arrivals[i] - blk * count
        return tuple(jnp.where(owner == n, i, was) for n, was in enumerate(found))

    found = lax.fori_loop(0, arrivals.shape[0], look, (jnp.int32(0),) * count, unroll=8)
    head_of = lax.broadcasted_iota(jnp.int32, (heads, D), 0) // group
    slot = lax.broadcasted_iota(jnp.int32, (heads, slots), 1)
    scores, own_scores, new_values = [], [], []
    for n in range(count):
        away = (found[n] // head_count) ^ blk
        line = (away // members) * head_count + (lax.rem(found[n], head_count) ^ head_at)
        line = line * PAD_PARTS
        x = None
        for part, block in enumerate(near):
            start = pl.multiple_of(block.shape[0] - height + line, PAD_PARTS)
            y = block[pl.ds(start, PAD_PARTS), :]
            x = y if x is None else jnp.where(lax.rem(away, members) == part, y, x)
        x = x.astype(jnp.float32)
        turned = turn(x, tables[0, n : n + 1, :], tables[1, n : n + 1, :])
        turned = turned.astype(jnp.bfloat16).astype(jnp.float32)
        q = turned[:heads]
        wide = [jnp.where(head_of == kv, q, 0.0) for kv in range(kv_heads)]
        wide = jnp.concatenate(wide, axis=1).astype(jnp.bfloat16)
        new_key = jnp.zeros((heads, D), jnp.float32)
        new_value = jnp.zeros((heads, D), jnp.float32)
        for kv in range(kv_heads):
            key = turned[heads + kv : heads + kv + 1]
            value = x[heads + kv_heads + kv : heads + kv_heads + kv + 1]
            new_key = jnp.where(head_of == kv, key, new_key)
            new_value = jnp.where(head_of == kv, value, new_value)
        s = lax.dot_general(
            wide, cache[0, n], (((1,), (1,)), ((), ())), preferred_element_type=jnp.float32
        )
        scores.append(jnp.where(slot < lengths[n], s, HIDDEN))
        own_scores.append(q * new_key)
        new_values.append(new_value)
    s = jnp.concatenate(scores, axis=0)
    own_s = jnp.sum(jnp.concatenate(own_scores, axis=0), axis=1, keepdims=True)
    top = jnp.maximum(jnp.max(s, axis=1, keepdims=True), own_s)
    w = jnp.exp2((s - top) * LOG2_SCALE)
    own_w = jnp.exp2((own_s - top) * LOG2_SCALE)
    scale = 1.0 / (jnp.sum(w, axis=1, keepdims=True) + own_w)
    own_w = own_w.astype(jnp.bfloat16).astype(jnp.float32)
    for n in range(count):
        lines = slice(n * heads, (n + 1) * heads)
        mix = jnp.dot(
            w[lines].astype(jnp.bfloat16), cache[1, n], preferred_element_type=jnp.float32
        )
        picked = own_w[lines] * new_values[n]
        for kv in range(kv_heads):
            picked = picked + jnp.where(head_of == kv, mix[:, kv * D : (kv + 1) * D], 0.0)
        picked = picked * scale[lines]
        for head in range(heads):
            mixed[n : n + 1, head * D : (head + 1) * D] = picked[head : head + 1, :]
    out[...] = mixed[...].astype(out.dtype)


def finish_kernel(
    lengths, arrivals, own, first, second, third, *refs
):
    rows, (cache, tables, long_out, dec_out, mixed, held) = refs[:-6], refs[-6:]
    low = 0
    for block in rows:
        held[low : low + block.shape[0], :] = block[...]
        low += block.shape[0]
    decode(lengths, arrivals, (held, first, second, third), cache, tables, dec_out, mixed)
    combine(own, first, second, third, long_out)


def after(block, *others):
    return lax.optimization_barrier((block, *others))[0]


def exchange(block, axis, distance):
    count = lax.axis_size(axis)
    return lax.ppermute(block, axis, [(i, i ^ distance) for i in range(count)])


NEAR = pl.BlockSpec(memory_space=pltpu.VMEM)
FAR = pl.BlockSpec(memory_space=pltpu.MemorySpace.HBM)
def stay(*arrays):
    return [pltpu.with_memory_space_constraint(a, pltpu.MemorySpace.HBM) for a in arrays]


SCALARS = pl.BlockSpec(memory_space=pltpu.SMEM)


def shards(
    long_query,
    long_new_kv,
    sink_kv,
    window,
    long_len,
    long_offset,
    dec_query,
    dec_new_kv,
    dec_cache,
    dec_len,
    arrival_order,
):
    blk_count, head_count = lax.axis_size("blk"), lax.axis_size("head")
    rows, features = long_query.shape
    heads = features // D
    kv_width = long_new_kv.shape[2]
    kv_heads = kv_width // D
    group = heads // kv_heads
    slots = window.shape[1]
    members = SPAN // rows
    own_count = dec_cache.shape[1]

    queries = {part: exchange(long_query, "blk", part) for part in range(1, members)}

    half = jnp.arange(D, dtype=jnp.int32) % (D // 2)
    frequency = (10000.0 ** (-(half.astype(jnp.float32) * 2.0 / D))).reshape(1, D)

    def call(kernel, out_shape, operands, specs, scratch, aliases={}):
        return pl.pallas_call(
            kernel,
            in_specs=specs,
            out_specs=jax.tree.map(lambda _: NEAR, out_shape),
            out_shape=out_shape,
            scratch_shapes=scratch,
            input_output_aliases=aliases,
            compiler_params=VMEM,
        )(*operands)

    pieces = call(
        spread_kernel,
        (jax.ShapeDtypeStruct((PAD_PARTS, D), jnp.bfloat16),) * head_count,
        stay(dec_query, dec_new_kv),
        [FAR, FAR],
        [
            pltpu.VMEM(dec_query.shape, jnp.bfloat16),
            pltpu.VMEM(dec_new_kv.shape, jnp.bfloat16),
            pltpu.SemaphoreType.DMA((2,)),
        ],
    )
    arrived = jnp.concatenate(
        [exchange(piece, "head", r) if r else piece for r, piece in enumerate(pieces)], axis=0
    )
    total = slots + rows + D
    shared = call(
        prepare_kernel,
        (
            jax.ShapeDtypeStruct((total, kv_width), jnp.bfloat16),
            jax.ShapeDtypeStruct((kv_width, total), jnp.bfloat16),
            jax.ShapeDtypeStruct((members, rows, D), jnp.float32),
            jax.ShapeDtypeStruct((members, rows, D), jnp.float32),
            jax.ShapeDtypeStruct((members, total, rows), jnp.float32),
            jax.ShapeDtypeStruct((2, -(-own_count // 8) * 8, D), jnp.float32),
        ),
        (*stay(long_len, long_offset, long_new_kv, sink_kv, window, dec_len), frequency),
        [FAR] * 6 + [NEAR],
        [
            pltpu.SMEM(long_len.shape, jnp.int32),
            pltpu.SMEM(long_offset.shape, jnp.int32),
            pltpu.SMEM(dec_len.shape, jnp.int32),
            pltpu.VMEM(long_new_kv.shape, jnp.bfloat16),
            pltpu.VMEM((2, *sink_kv.shape[2:]), jnp.bfloat16),
            pltpu.VMEM(window.shape[1:], jnp.bfloat16),
            pltpu.VMEM((D, kv_width), jnp.float32),
            pltpu.SemaphoreType.DMA((7,)),
        ],
    )

    def attend(part, query, spare, *passenger):
        if part == 0:
            out = jax.ShapeDtypeStruct((features + heads, rows), jnp.float32)
        else:
            lines = features + LOG_LINES * heads + spare
            lines += sum(p.shape[0] for p in passenger)
            out = jax.ShapeDtypeStruct((lines, rows), jnp.bfloat16)
        return call(
            functools.partial(attend_kernel, part),
            out,
            (query, *shared[:5], *passenger),
            [NEAR] * (6 + len(passenger)),
            [
                pltpu.VMEM((kv_heads, total, group * rows), jnp.float32),
                pltpu.VMEM((kv_heads, total, group * rows), jnp.bfloat16),
            ],
        )

    arrived = after(arrived, shared[0])
    blocks, distance = [arrived], members
    while distance < blk_count:
        full = blocks[0] if len(blocks) == 1 else jnp.concatenate(blocks, axis=0)
        blocks = [full, exchange(full, "blk", distance)]
        distance *= 2
    spare = sum(block.shape[0] for block in blocks)
    mine = attend(0, long_query, 0)
    backs = {}
    for part in range(1, members):
        if part == members - 1:
            mix = attend(part, queries[part], spare)
            mix = call(
                append_kernel,
                jax.ShapeDtypeStruct(mix.shape, mix.dtype),
                (mix, *blocks),
                [NEAR] * (1 + len(blocks)),
                [],
                {0: 0},
            )
        else:
            mix = attend(part, queries[part], 0, *blocks)
        backs[part] = exchange(mix, "blk", part)
    first_back, second_back, third_back = [backs[part] for part in range(1, members)]
    return call(
        finish_kernel,
        (
            jax.ShapeDtypeStruct((rows, features), jnp.bfloat16),
            jax.ShapeDtypeStruct((own_count, features), jnp.bfloat16),
        ),
        (
            dec_len, arrival_order, mine, first_back, second_back, third_back,
            *blocks, dec_cache, shared[5],
        ),
        [SCALARS, SCALARS] + [NEAR] * (6 + len(blocks)),
        [
            pltpu.VMEM((own_count, features), jnp.float32),
            pltpu.VMEM((spare, D), jnp.bfloat16),
        ],
    )


def solution(mesh):
    in_specs = (
        P("blk", "head"),
        P(None, "blk", "head"),
        P(None, None, None, "head"),
        P(None, "blk", "head"),
        P(),
        P(),
        P(("blk", "head"), None),
        P(("blk", "head"), None, None),
        P(None, "blk", None, "head"),
        P("blk"),
        P(),
    )
    out_specs = (P("blk", "head"), P("blk", "head"))
    return jax.shard_map(shards, mesh=mesh, in_specs=in_specs, out_specs=out_specs, check_vma=False)
```

```python
import functools
import math

import jax
import jax.numpy as jnp
from jax import lax
from jax.experimental import pallas as pl
from jax.experimental.pallas import tpu as pltpu
from jax.sharding import PartitionSpec as P

D = 128
W = 4096
SINKS = 4
SPAN = 512
PAD_PARTS = 16
LOG_LINES = 4
HIDDEN = -1e30
LOG2_SCALE = math.log2(math.e) / math.sqrt(D)
VMEM = pltpu.CompilerParams(vmem_limit_bytes=24 * 1024 * 1024)


def turn(x, cosine, sine):
    return x * cosine + pltpu.roll(x, D // 2, 1) * sine


def split_three(x):
    high = x.astype(jnp.bfloat16)
    rest = x - high.astype(jnp.float32)
    middle = rest.astype(jnp.bfloat16)
    low = (rest - middle.astype(jnp.float32)).astype(jnp.bfloat16)
    return high, middle, low


def angle_tables(length, first_step, frequency):
    half = D // 2
    line = lax.broadcasted_iota(jnp.int32, (half, D), 0)
    lane = lax.broadcasted_iota(jnp.int32, (half, D), 1)
    low = lane < half
    position = length + first_step + line + jnp.where(low, 0, half)
    angle = position.astype(jnp.float32) * frequency
    cosine, sine = jnp.cos(angle), jnp.sin(angle)
    cosine_r, sine_r = pltpu.roll(cosine, half, 1), pltpu.roll(sine, half, 1)
    cosines = [jnp.where(low, cosine, cosine_r), jnp.where(low, cosine_r, cosine)]
    sines = [jnp.where(low, -sine, sine_r), jnp.where(low, -sine_r, sine)]
    return jnp.concatenate(cosines, axis=0), jnp.concatenate(sines, axis=0)


def whereabouts(rows):
    members = SPAN // rows
    blk = lax.axis_index("blk")
    return blk // members, lax.rem(blk, members)


def fetch(*pairs):
    copies = [pltpu.make_async_copy(*pair) for pair in pairs]
    for copy in copies:
        copy.start()
    return copies


def spread_kernel(query_far, new_kv_far, *refs):
    pieces, (query, new_kv, arrived) = refs[:-3], refs[-3:]
    for copy in fetch(
        (query_far, query, arrived.at[0]), (new_kv_far, new_kv, arrived.at[1])
    ):
        copy.wait()
    head_at = lax.axis_index("head")
    width = query.shape[1] // len(pieces)
    kv_width = new_kv.shape[2] // len(pieces)

    def lines(ref, size, at):
        found = ref[:, pl.ds(pl.multiple_of(at * size, D), size)].astype(jnp.float32)
        return [
            found[line : line + 1, low : low + D]
            for line in range(found.shape[0])
            for low in range(0, size, D)
        ]

    for distance, piece in enumerate(pieces):
        at = head_at ^ distance
        found = lines(query, width, at) + lines(new_kv.at[0], kv_width, at)
        found.append(jnp.zeros((PAD_PARTS - len(found), D), jnp.float32))
        piece[...] = jnp.concatenate(found, axis=0).astype(piece.dtype)


def prepare_kernel(
    lengths_far,
    offsets_far,
    new_kv_far,
    sinks_far,
    window_far,
    dec_lengths_far,
    frequency,
    keys,
    values_t,
    cosines,
    sines,
    biases,
    dec_tables,
    lengths,
    offsets,
    dec_lengths,
    new_kv,
    sinks,
    values,
    pad,
    arrived,
):
    rows = new_kv.shape[1]
    slots = values.shape[0]
    request, place = whereabouts(rows)
    scalars = fetch(
        (lengths_far, lengths, arrived.at[0]),
        (offsets_far, offsets, arrived.at[1]),
        (dec_lengths_far, dec_lengths, arrived.at[6]),
    )
    arrays = fetch(
        (new_kv_far, new_kv, arrived.at[2]),
        (sinks_far.at[:, request], sinks, arrived.at[3]),
        (window_far.at[1], values, arrived.at[4]),
        (window_far.at[0], keys.at[:slots], arrived.at[5]),
    )
    for copy in scalars:
        copy.wait()
    length, offset = lengths[request], offsets[request]
    filled = jnp.minimum(length - SINKS, W)
    for part in range(cosines.shape[0]):
        first_step = (place ^ part) * rows
        for low in range(0, rows, D):
            lines = slice(low, low + D)
            cosines[part, lines], sines[part, lines] = angle_tables(
                length, first_step + low, frequency[...]
            )
    line = lax.broadcasted_iota(jnp.int32, dec_tables.shape[1:], 0)
    lane = lax.broadcasted_iota(jnp.int32, dec_tables.shape[1:], 1)
    position = jnp.zeros(dec_tables.shape[1:], jnp.int32)
    for n in range(dec_lengths.shape[0]):
        position = jnp.where(line == n, dec_lengths[n], position)
    angle = position.astype(jnp.float32) * frequency[...]
    sine = jnp.sin(angle)
    dec_tables[0] = jnp.cos(angle)
    dec_tables[1] = jnp.where(lane < D // 2, -sine, sine)
    index = lax.broadcasted_iota(jnp.int32, (D, rows), 0)
    step = lax.broadcasted_iota(jnp.int32, (D, rows), 1)
    for low in range(0, slots, D):
        age = (place * slots + low - offset + index) & (W - 1)
        limit = jnp.where(age < filled, age - filled + W, -1)
        for part in range(biases.shape[0]):
            seen = limit > (place ^ part) * rows + step
            biases[part, low : low + D] = jnp.where(seen, 0.0, HIDDEN)
    for low in range(0, rows, D):
        for part in range(biases.shape[0]):
            seen = place * rows + low + index <= (place ^ part) * rows + step
            biases[part, slots + low : slots + low + D] = jnp.where(seen, 0.0, HIDDEN)
    for part in range(biases.shape[0]):
        seen = index < (SINKS if part == 0 else 0)
        biases[part, slots + rows :] = jnp.where(seen, 0.0, HIDDEN)
    for copy in arrays:
        copy.wait()
    for head in range(new_kv.shape[2] // D):
        lanes = slice(head * D, (head + 1) * D)
        key = turn(new_kv[0, :, lanes].astype(jnp.float32), cosines[0], sines[0])
        keys[slots : slots + rows, lanes] = key.astype(jnp.bfloat16)
    for kind in range(2):
        pad[...] = jnp.zeros_like(pad)
        pad[:SINKS, :] = sinks[kind].astype(jnp.float32)
        if kind == 0:
            keys[slots + rows :, :] = pad[...].astype(jnp.bfloat16)
        else:
            values_t[:, slots + rows :] = pad[...].T.astype(jnp.bfloat16)
    values_t[:, :slots] = values[...].T
    values_t[:, slots : slots + rows] = new_kv[1].T


def attend_kernel(part, query, keys, values_t, cosine, sine, bias, *refs):
    own = part == 0
    passengers, (out, scores, weights) = refs[:-3], refs[-3:]
    rows = query.shape[0]
    kv_heads = keys.shape[1] // D
    group = query.shape[1] // D // kv_heads
    total = keys.shape[0] if own else keys.shape[0] - D
    share = group
    heads = kv_heads * group
    units = heads // share
    blocks, tops, masses, logs = {}, {}, {}, []

    def score_unit(unit, low):
        kv = unit
        lanes = slice(kv * D, (kv + 1) * D)
        if low == 0:
            turned = []
            for head in range(unit * share, (unit + 1) * share):
                x = query[:, head * D : (head + 1) * D].astype(jnp.float32)
                turned.append(turn(x, cosine[part], sine[part]).astype(jnp.bfloat16))
            blocks[unit] = jnp.concatenate(turned, axis=0)
        s = lax.dot_general(
            keys[low : low + D, lanes],
            blocks[unit],
            (((1,), (1,)), ((), ())),
            preferred_element_type=jnp.float32,
        )
        s = s + jnp.concatenate([bias[part, low : low + D]] * share, axis=1)
        scores[unit, low : low + D, :] = s
        peak = jnp.max(s.reshape(D // 8, 8, share * rows), axis=0)
        tops[unit] = peak if low == 0 else jnp.maximum(tops[unit], peak)

    def weigh_unit(unit, low):
        if low == 0:
            tops[unit] = jnp.max(tops[unit], axis=0, keepdims=True)
        w = jnp.exp2((scores[unit, low : low + D, :] - tops[unit]) * LOG2_SCALE)
        mass = jnp.sum(w.reshape(D // 8, 8, share * rows), axis=0)
        masses[unit] = mass if low == 0 else masses[unit] + mass
        weights[unit, low : low + D, :] = w.astype(jnp.bfloat16)

    def finish_unit(unit):
        kv = unit
        mass = jnp.sum(masses[unit], axis=0, keepdims=True)
        mix = jnp.dot(
            values_t[kv * D : (kv + 1) * D, :total],
            weights[unit, :total, :],
            preferred_element_type=jnp.float32,
        )
        mix = mix * (1.0 / mass)
        log = tops[unit] * LOG2_SCALE + jnp.log2(mass)
        for j in range(share):
            head = unit * share + j
            out[head * D : (head + 1) * D, :] = mix[:, j * rows : (j + 1) * rows].astype(out.dtype)
            logs.append(log[:, j * rows : (j + 1) * rows])

    for step in range(units + 2):
        if step >= 2:
            finish_unit(step - 2)
        for low in range(0, total, D):
            if step < units:
                score_unit(step, low)
            if 1 <= step <= units:
                weigh_unit(step - 1, low)
    log = jnp.concatenate(logs, axis=0)
    if own:
        out[heads * D :, :] = log
    else:
        pieces = [p.astype(jnp.float32) for p in split_three(log)]
        pieces.append(jnp.zeros_like(log))
        end = heads * D + LOG_LINES * heads
        out[heads * D : end, :] = jnp.concatenate(pieces, axis=0).astype(out.dtype)
        for block in passengers:
            out[end : end + block.shape[0], :] = block[...]
            end += block.shape[0]


def append_kernel(block, *refs):
    passengers, out = refs[:-1], refs[-1]
    end = block.shape[0]
    for passenger in passengers[::-1]:
        out[end - passenger.shape[0] : end, :] = passenger[...]
        end -= passenger.shape[0]


def combine(own, first, second, third, out):
    heads = out.shape[1] // D
    logs = [own[heads * D :, :]]
    for other in (first, second, third):
        p = other[heads * D : (D + LOG_LINES) * heads, :].astype(jnp.float32)
        logs.append(p[:heads] + p[heads : 2 * heads] + p[2 * heads : 3 * heads])
    top = functools.reduce(jnp.maximum, logs)
    shares = [jnp.exp2(log - top) for log in logs]
    scale = 1.0 / sum(shares)
    shares = [share * scale for share in shares]
    for head in range(heads):
        lines = slice(head * D, (head + 1) * D)
        mix = own[lines, :] * shares[0][head : head + 1, :]
        for other, share in zip((first, second, third), shares[1:]):
            mix = mix + other[lines, :].astype(jnp.float32) * share[head : head + 1, :]
        out[:, lines] = mix.T.astype(out.dtype)


def decode(lengths, arrivals, near, cache, tables, out, mixed):
    count = cache.shape[1]
    slots = cache.shape[2]
    kv_heads = cache.shape[3] // D
    heads = out.shape[1] // D
    group = heads // kv_heads
    blk, head_at = lax.axis_index("blk"), lax.axis_index("head")
    head_count = lax.axis_size("head")
    members = len(near)
    height = near[0].shape[0]

    def look(i, found):
        owner = arrivals[i] - blk * count
        return tuple(jnp.where(owner == n, i, was) for n, was in enumerate(found))

    found = lax.fori_loop(0, arrivals.shape[0], look, (jnp.int32(0),) * count, unroll=min(32, arrivals.shape[0]))
    head_of = lax.broadcasted_iota(jnp.int32, (heads, D), 0) // group
    slot = lax.broadcasted_iota(jnp.int32, (heads, slots), 1)
    scores, own_scores, new_values = [], [], []
    for n in range(count):
        away = (found[n] // head_count) ^ blk
        line = (away // members) * head_count + (lax.rem(found[n], head_count) ^ head_at)
        line = line * PAD_PARTS
        x = None
        for part, block in enumerate(near):
            start = pl.multiple_of(block.shape[0] - height + line, PAD_PARTS)
            y = block[pl.ds(start, PAD_PARTS), :]
            x = y if x is None else jnp.where(lax.rem(away, members) == part, y, x)
        x = x.astype(jnp.float32)
        turned = turn(x, tables[0, n : n + 1, :], tables[1, n : n + 1, :])
        turned = turned.astype(jnp.bfloat16).astype(jnp.float32)
        q = turned[:heads]
        wide = [jnp.where(head_of == kv, q, 0.0) for kv in range(kv_heads)]
        wide = jnp.concatenate(wide, axis=1).astype(jnp.bfloat16)
        new_key = jnp.zeros((heads, D), jnp.float32)
        new_value = jnp.zeros((heads, D), jnp.float32)
        for kv in range(kv_heads):
            key = turned[heads + kv : heads + kv + 1]
            value = x[heads + kv_heads + kv : heads + kv_heads + kv + 1]
            new_key = jnp.where(head_of == kv, key, new_key)
            new_value = jnp.where(head_of == kv, value, new_value)
        s = lax.dot_general(
            wide, cache[0, n], (((1,), (1,)), ((), ())), preferred_element_type=jnp.float32
        )
        scores.append(jnp.where(slot < lengths[n], s, HIDDEN))
        own_scores.append(q * new_key)
        new_values.append(new_value)
    s = jnp.concatenate(scores, axis=0)
    own_s = jnp.sum(jnp.concatenate(own_scores, axis=0), axis=1, keepdims=True)
    top = jnp.maximum(jnp.max(s, axis=1, keepdims=True), own_s)
    w = jnp.exp2((s - top) * LOG2_SCALE)
    own_w = jnp.exp2((own_s - top) * LOG2_SCALE)
    scale = 1.0 / (jnp.sum(w, axis=1, keepdims=True) + own_w)
    own_w = own_w.astype(jnp.bfloat16).astype(jnp.float32)
    for n in range(count):
        lines = slice(n * heads, (n + 1) * heads)
        mix = jnp.dot(
            w[lines].astype(jnp.bfloat16), cache[1, n], preferred_element_type=jnp.float32
        )
        picked = own_w[lines] * new_values[n]
        for kv in range(kv_heads):
            picked = picked + jnp.where(head_of == kv, mix[:, kv * D : (kv + 1) * D], 0.0)
        picked = picked * scale[lines]
        for head in range(heads):
            mixed[n : n + 1, head * D : (head + 1) * D] = picked[head : head + 1, :]
    out[...] = mixed[...].astype(out.dtype)


def finish_kernel(
    lengths, arrivals, own, first, second, third, *refs
):
    rows, (cache, tables, long_out, dec_out, mixed, held) = refs[:-6], refs[-6:]
    low = 0
    for block in rows:
        held[low : low + block.shape[0], :] = block[...]
        low += block.shape[0]
    decode(lengths, arrivals, (held, first, second, third), cache, tables, dec_out, mixed)
    combine(own, first, second, third, long_out)


def after(block, *others):
    return lax.optimization_barrier((block, *others))[0]


def exchange(block, axis, distance):
    count = lax.axis_size(axis)
    return lax.ppermute(block, axis, [(i, i ^ distance) for i in range(count)])


NEAR = pl.BlockSpec(memory_space=pltpu.VMEM)
FAR = pl.BlockSpec(memory_space=pltpu.MemorySpace.HBM)
def stay(*arrays):
    return [pltpu.with_memory_space_constraint(a, pltpu.MemorySpace.HBM) for a in arrays]


SCALARS = pl.BlockSpec(memory_space=pltpu.SMEM)


def shards(
    long_query,
    long_new_kv,
    sink_kv,
    window,
    long_len,
    long_offset,
    dec_query,
    dec_new_kv,
    dec_cache,
    dec_len,
    arrival_order,
):
    blk_count, head_count = lax.axis_size("blk"), lax.axis_size("head")
    rows, features = long_query.shape
    heads = features // D
    kv_width = long_new_kv.shape[2]
    kv_heads = kv_width // D
    group = heads // kv_heads
    slots = window.shape[1]
    members = SPAN // rows
    own_count = dec_cache.shape[1]

    queries = {part: exchange(long_query, "blk", part) for part in range(1, members)}

    half = jnp.arange(D, dtype=jnp.int32) % (D // 2)
    frequency = (10000.0 ** (-(half.astype(jnp.float32) * 2.0 / D))).reshape(1, D)

    def call(kernel, out_shape, operands, specs, scratch, aliases={}):
        return pl.pallas_call(
            kernel,
            in_specs=specs,
            out_specs=jax.tree.map(lambda _: NEAR, out_shape),
            out_shape=out_shape,
            scratch_shapes=scratch,
            input_output_aliases=aliases,
            compiler_params=VMEM,
        )(*operands)

    pieces = call(
        spread_kernel,
        (jax.ShapeDtypeStruct((PAD_PARTS, D), jnp.bfloat16),) * head_count,
        stay(dec_query, dec_new_kv),
        [FAR, FAR],
        [
            pltpu.VMEM(dec_query.shape, jnp.bfloat16),
            pltpu.VMEM(dec_new_kv.shape, jnp.bfloat16),
            pltpu.SemaphoreType.DMA((2,)),
        ],
    )
    arrived = jnp.concatenate(
        [exchange(piece, "head", r) if r else piece for r, piece in enumerate(pieces)], axis=0
    )
    total = slots + rows + D
    shared = call(
        prepare_kernel,
        (
            jax.ShapeDtypeStruct((total, kv_width), jnp.bfloat16),
            jax.ShapeDtypeStruct((kv_width, total), jnp.bfloat16),
            jax.ShapeDtypeStruct((members, rows, D), jnp.float32),
            jax.ShapeDtypeStruct((members, rows, D), jnp.float32),
            jax.ShapeDtypeStruct((members, total, rows), jnp.float32),
            jax.ShapeDtypeStruct((2, -(-own_count // 8) * 8, D), jnp.float32),
        ),
        (*stay(long_len, long_offset, long_new_kv, sink_kv, window, dec_len), frequency),
        [FAR] * 6 + [NEAR],
        [
            pltpu.SMEM(long_len.shape, jnp.int32),
            pltpu.SMEM(long_offset.shape, jnp.int32),
            pltpu.SMEM(dec_len.shape, jnp.int32),
            pltpu.VMEM(long_new_kv.shape, jnp.bfloat16),
            pltpu.VMEM((2, *sink_kv.shape[2:]), jnp.bfloat16),
            pltpu.VMEM(window.shape[1:], jnp.bfloat16),
            pltpu.VMEM((D, kv_width), jnp.float32),
            pltpu.SemaphoreType.DMA((7,)),
        ],
    )

    def attend(part, query, spare, *passenger):
        if part == 0:
            out = jax.ShapeDtypeStruct((features + heads, rows), jnp.float32)
        else:
            lines = features + LOG_LINES * heads + spare
            lines += sum(p.shape[0] for p in passenger)
            out = jax.ShapeDtypeStruct((lines, rows), jnp.bfloat16)
        return call(
            functools.partial(attend_kernel, part),
            out,
            (query, *shared[:5], *passenger),
            [NEAR] * (6 + len(passenger)),
            [
                pltpu.VMEM((kv_heads, total, group * rows), jnp.float32),
                pltpu.VMEM((kv_heads, total, group * rows), jnp.bfloat16),
            ],
        )

    arrived = after(arrived, shared[0])
    blocks, distance = [arrived], members
    while distance < blk_count:
        full = blocks[0] if len(blocks) == 1 else jnp.concatenate(blocks, axis=0)
        blocks = [full, exchange(full, "blk", distance)]
        distance *= 2
    spare = sum(block.shape[0] for block in blocks)
    mine = attend(0, long_query, 0)
    backs = {}
    for part in range(1, members):
        if part == members - 1:
            mix = attend(part, queries[part], spare)
            mix = call(
                append_kernel,
                jax.ShapeDtypeStruct(mix.shape, mix.dtype),
                (mix, *blocks),
                [NEAR] * (1 + len(blocks)),
                [],
                {0: 0},
            )
        else:
            mix = attend(part, queries[part], 0, *blocks)
        backs[part] = exchange(mix, "blk", part)
    first_back, second_back, third_back = [backs[part] for part in range(1, members)]
    return call(
        finish_kernel,
        (
            jax.ShapeDtypeStruct((rows, features), jnp.bfloat16),
            jax.ShapeDtypeStruct((own_count, features), jnp.bfloat16),
        ),
        (
            dec_len, arrival_order, mine, first_back, second_back, third_back,
            *blocks, dec_cache, shared[5],
        ),
        [SCALARS, SCALARS] + [NEAR] * (6 + len(blocks)),
        [
            pltpu.VMEM((own_count, features), jnp.float32),
            pltpu.VMEM((spare, D), jnp.bfloat16),
        ],
    )


def solution(mesh):
    in_specs = (
        P("blk", "head"),
        P(None, "blk", "head"),
        P(None, None, None, "head"),
        P(None, "blk", "head"),
        P(),
        P(),
        P(("blk", "head"), None),
        P(("blk", "head"), None, None),
        P(None, "blk", None, "head"),
        P("blk"),
        P(),
    )
    out_specs = (P("blk", "head"), P("blk", "head"))
    return jax.shard_map(shards, mesh=mesh, in_specs=in_specs, out_specs=out_specs, check_vma=False)
```

```python
import functools
import math

import jax
import jax.numpy as jnp
from jax import lax
from jax.experimental import pallas as pl
from jax.experimental.pallas import tpu as pltpu
from jax.sharding import PartitionSpec as P

D = 128
W = 4096
SINKS = 4
SPAN = 512
PAD_PARTS = 16
LOG_LINES = 4
HIDDEN = -1e30
LOG2_SCALE = math.log2(math.e) / math.sqrt(D)
VMEM = pltpu.CompilerParams(vmem_limit_bytes=24 * 1024 * 1024)


def turn(x, cosine, sine):
    return x * cosine + pltpu.roll(x, D // 2, 1) * sine


def split_three(x):
    high = x.astype(jnp.bfloat16)
    rest = x - high.astype(jnp.float32)
    middle = rest.astype(jnp.bfloat16)
    low = (rest - middle.astype(jnp.float32)).astype(jnp.bfloat16)
    return high, middle, low


def angle_tables(length, first_step, frequency):
    half = D // 2
    line = lax.broadcasted_iota(jnp.int32, (half, D), 0)
    lane = lax.broadcasted_iota(jnp.int32, (half, D), 1)
    low = lane < half
    position = length + first_step + line + jnp.where(low, 0, half)
    angle = position.astype(jnp.float32) * frequency
    cosine, sine = jnp.cos(angle), jnp.sin(angle)
    cosine_r, sine_r = pltpu.roll(cosine, half, 1), pltpu.roll(sine, half, 1)
    cosines = [jnp.where(low, cosine, cosine_r), jnp.where(low, cosine_r, cosine)]
    sines = [jnp.where(low, -sine, sine_r), jnp.where(low, -sine_r, sine)]
    return jnp.concatenate(cosines, axis=0), jnp.concatenate(sines, axis=0)


def whereabouts(rows):
    members = SPAN // rows
    blk = lax.axis_index("blk")
    return blk // members, lax.rem(blk, members)


def fetch(*pairs):
    copies = [pltpu.make_async_copy(*pair) for pair in pairs]
    for copy in copies:
        copy.start()
    return copies


def spread_kernel(query_far, new_kv_far, *refs):
    pieces, (query, new_kv, arrived) = refs[:-3], refs[-3:]
    for copy in fetch(
        (query_far, query, arrived.at[0]), (new_kv_far, new_kv, arrived.at[1])
    ):
        copy.wait()
    head_at = lax.axis_index("head")
    width = query.shape[1] // len(pieces)
    kv_width = new_kv.shape[2] // len(pieces)

    def lines(ref, size, at):
        found = ref[:, pl.ds(pl.multiple_of(at * size, D), size)].astype(jnp.float32)
        return [
            found[line : line + 1, low : low + D]
            for line in range(found.shape[0])
            for low in range(0, size, D)
        ]

    for distance, piece in enumerate(pieces):
        at = head_at ^ distance
        found = lines(query, width, at) + lines(new_kv.at[0], kv_width, at)
        found.append(jnp.zeros((PAD_PARTS - len(found), D), jnp.float32))
        piece[...] = jnp.concatenate(found, axis=0).astype(piece.dtype)


def prepare_kernel(
    lengths_far,
    offsets_far,
    new_kv_far,
    sinks_far,
    window_far,
    dec_lengths_far,
    frequency,
    keys,
    values_t,
    cosines,
    sines,
    biases,
    dec_tables,
    lengths,
    offsets,
    dec_lengths,
    new_kv,
    sinks,
    values,
    pad,
    arrived,
):
    rows = new_kv.shape[1]
    slots = values.shape[0]
    request, place = whereabouts(rows)
    scalars = fetch(
        (lengths_far, lengths, arrived.at[0]),
        (offsets_far, offsets, arrived.at[1]),
        (dec_lengths_far, dec_lengths, arrived.at[6]),
    )
    arrays = fetch(
        (new_kv_far, new_kv, arrived.at[2]),
        (sinks_far.at[:, request], sinks, arrived.at[3]),
        (window_far.at[1], values, arrived.at[4]),
        (window_far.at[0], keys.at[:slots], arrived.at[5]),
    )
    for copy in scalars:
        copy.wait()
    length, offset = lengths[request], offsets[request]
    filled = jnp.minimum(length - SINKS, W)
    for part in range(cosines.shape[0]):
        first_step = (place ^ part) * rows
        for low in range(0, rows, D):
            lines = slice(low, low + D)
            cosines[part, lines], sines[part, lines] = angle_tables(
                length, first_step + low, frequency[...]
            )
    line = lax.broadcasted_iota(jnp.int32, dec_tables.shape[1:], 0)
    lane = lax.broadcasted_iota(jnp.int32, dec_tables.shape[1:], 1)
    position = jnp.zeros(dec_tables.shape[1:], jnp.int32)
    for n in range(dec_lengths.shape[0]):
        position = jnp.where(line == n, dec_lengths[n], position)
    angle = position.astype(jnp.float32) * frequency[...]
    sine = jnp.sin(angle)
    dec_tables[0] = jnp.cos(angle)
    dec_tables[1] = jnp.where(lane < D // 2, -sine, sine)
    index = lax.broadcasted_iota(jnp.int32, (D, rows), 0)
    step = lax.broadcasted_iota(jnp.int32, (D, rows), 1)
    for low in range(0, slots, D):
        age = (place * slots + low - offset + index) & (W - 1)
        limit = jnp.where(age < filled, age - filled + W, -1)
        for part in range(biases.shape[0]):
            seen = limit > (place ^ part) * rows + step
            biases[part, low : low + D] = jnp.where(seen, 0.0, HIDDEN)
    for low in range(0, rows, D):
        for part in range(biases.shape[0]):
            seen = place * rows + low + index <= (place ^ part) * rows + step
            biases[part, slots + low : slots + low + D] = jnp.where(seen, 0.0, HIDDEN)
    for part in range(biases.shape[0]):
        seen = index < (SINKS if part == 0 else 0)
        biases[part, slots + rows :] = jnp.where(seen, 0.0, HIDDEN)
    for copy in arrays:
        copy.wait()
    for head in range(new_kv.shape[2] // D):
        lanes = slice(head * D, (head + 1) * D)
        key = turn(new_kv[0, :, lanes].astype(jnp.float32), cosines[0], sines[0])
        keys[slots : slots + rows, lanes] = key.astype(jnp.bfloat16)
    for kind in range(2):
        pad[...] = jnp.zeros_like(pad)
        pad[:SINKS, :] = sinks[kind].astype(jnp.float32)
        if kind == 0:
            keys[slots + rows :, :] = pad[...].astype(jnp.bfloat16)
        else:
            values_t[:, slots + rows :] = pad[...].T.astype(jnp.bfloat16)
    values_t[:, :slots] = values[...].T
    values_t[:, slots : slots + rows] = new_kv[1].T


def attend_kernel(part, query, keys, values_t, cosine, sine, bias, *refs):
    own = part == 0
    passengers, (out, scores, weights) = refs[:-3], refs[-3:]
    rows = query.shape[0]
    kv_heads = keys.shape[1] // D
    group = query.shape[1] // D // kv_heads
    total = keys.shape[0] if own else keys.shape[0] - D
    share = group
    heads = kv_heads * group
    units = heads // share
    blocks, tops, masses, logs = {}, {}, {}, []

    def score_unit(unit, low):
        kv = unit
        lanes = slice(kv * D, (kv + 1) * D)
        if low == 0:
            turned = []
            for head in range(unit * share, (unit + 1) * share):
                x = query[:, head * D : (head + 1) * D].astype(jnp.float32)
                turned.append(turn(x, cosine[part], sine[part]).astype(jnp.bfloat16))
            blocks[unit] = jnp.concatenate(turned, axis=0)
        s = lax.dot_general(
            keys[low : low + D, lanes],
            blocks[unit],
            (((1,), (1,)), ((), ())),
            preferred_element_type=jnp.float32,
        )
        s = s + jnp.concatenate([bias[part, low : low + D]] * share, axis=1)
        scores[unit, low : low + D, :] = s
        peak = jnp.max(s.reshape(D // 8, 8, share * rows), axis=0)
        tops[unit] = peak if low == 0 else jnp.maximum(tops[unit], peak)

    def weigh_unit(unit, low):
        if low == 0:
            tops[unit] = jnp.max(tops[unit], axis=0, keepdims=True)
        w = jnp.exp2((scores[unit, low : low + D, :] - tops[unit]) * LOG2_SCALE)
        mass = jnp.sum(w.reshape(D // 8, 8, share * rows), axis=0)
        masses[unit] = mass if low == 0 else masses[unit] + mass
        weights[unit, low : low + D, :] = w.astype(jnp.bfloat16)

    def finish_unit(unit):
        kv = unit
        mass = jnp.sum(masses[unit], axis=0, keepdims=True)
        mix = jnp.dot(
            values_t[kv * D : (kv + 1) * D, :total],
            weights[unit, :total, :],
            preferred_element_type=jnp.float32,
        )
        mix = mix * (1.0 / mass)
        log = tops[unit] * LOG2_SCALE + jnp.log2(mass)
        for j in range(share):
            head = unit * share + j
            out[head * D : (head + 1) * D, :] = mix[:, j * rows : (j + 1) * rows].astype(out.dtype)
            logs.append(log[:, j * rows : (j + 1) * rows])

    for step in range(units + 2):
        if step >= 2:
            finish_unit(step - 2)
        for low in range(0, total, D):
            if step < units:
                score_unit(step, low)
            if 1 <= step <= units:
                weigh_unit(step - 1, low)
    log = jnp.concatenate(logs, axis=0)
    if own:
        out[heads * D :, :] = log
    else:
        pieces = [p.astype(jnp.float32) for p in split_three(log)]
        pieces.append(jnp.zeros_like(log))
        end = heads * D + LOG_LINES * heads
        out[heads * D : end, :] = jnp.concatenate(pieces, axis=0).astype(out.dtype)
        for block in passengers:
            out[end : end + block.shape[0], :] = block[...]
            end += block.shape[0]


def append_kernel(block, *refs):
    passengers, out = refs[:-1], refs[-1]
    end = block.shape[0]
    for passenger in passengers[::-1]:
        out[end - passenger.shape[0] : end, :] = passenger[...]
        end -= passenger.shape[0]


def combine(own, first, second, third, out):
    heads = out.shape[1] // D
    logs = [own[heads * D :, :]]
    for other in (first, second, third):
        p = other[heads * D : (D + LOG_LINES) * heads, :].astype(jnp.float32)
        logs.append(p[:heads] + p[heads : 2 * heads] + p[2 * heads : 3 * heads])
    top = functools.reduce(jnp.maximum, logs)
    shares = [jnp.exp2(log - top) for log in logs]
    scale = 1.0 / sum(shares)
    shares = [share * scale for share in shares]
    for head in range(heads):
        lines = slice(head * D, (head + 1) * D)
        mix = own[lines, :] * shares[0][head : head + 1, :]
        for other, share in zip((first, second, third), shares[1:]):
            mix = mix + other[lines, :].astype(jnp.float32) * share[head : head + 1, :]
        out[:, lines] = mix.astype(out.dtype).T


def decode(lengths, arrivals, near, cache, tables, out, mixed):
    count = cache.shape[1]
    slots = cache.shape[2]
    kv_heads = cache.shape[3] // D
    heads = out.shape[1] // D
    group = heads // kv_heads
    blk, head_at = lax.axis_index("blk"), lax.axis_index("head")
    head_count = lax.axis_size("head")
    members = len(near)
    height = near[0].shape[0]

    def look(i, found):
        owner = arrivals[i] - blk * count
        return tuple(jnp.where(owner == n, i, was) for n, was in enumerate(found))

    found = lax.fori_loop(0, arrivals.shape[0], look, (jnp.int32(0),) * count, unroll=min(32, arrivals.shape[0]))
    head_of = lax.broadcasted_iota(jnp.int32, (heads, D), 0) // group
    slot = lax.broadcasted_iota(jnp.int32, (heads, slots), 1)
    scores, own_scores, new_values = [], [], []
    for n in range(count):
        away = (found[n] // head_count) ^ blk
        line = (away // members) * head_count + (lax.rem(found[n], head_count) ^ head_at)
        line = line * PAD_PARTS
        x = None
        for part, block in enumerate(near):
            start = pl.multiple_of(block.shape[0] - height + line, PAD_PARTS)
            y = block[pl.ds(start, PAD_PARTS), :]
            x = y if x is None else jnp.where(lax.rem(away, members) == part, y, x)
        x = x.astype(jnp.float32)
        turned = turn(x, tables[0, n : n + 1, :], tables[1, n : n + 1, :])
        turned = turned.astype(jnp.bfloat16).astype(jnp.float32)
        q = turned[:heads]
        wide = [jnp.where(head_of == kv, q, 0.0) for kv in range(kv_heads)]
        wide = jnp.concatenate(wide, axis=1).astype(jnp.bfloat16)
        new_key = jnp.zeros((heads, D), jnp.float32)
        new_value = jnp.zeros((heads, D), jnp.float32)
        for kv in range(kv_heads):
            key = turned[heads + kv : heads + kv + 1]
            value = x[heads + kv_heads + kv : heads + kv_heads + kv + 1]
            new_key = jnp.where(head_of == kv, key, new_key)
            new_value = jnp.where(head_of == kv, value, new_value)
        s = lax.dot_general(
            wide, cache[0, n], (((1,), (1,)), ((), ())), preferred_element_type=jnp.float32
        )
        scores.append(jnp.where(slot < lengths[n], s, HIDDEN))
        own_scores.append(q * new_key)
        new_values.append(new_value)
    s = jnp.concatenate(scores, axis=0)
    own_s = jnp.sum(jnp.concatenate(own_scores, axis=0), axis=1, keepdims=True)
    top = jnp.maximum(jnp.max(s, axis=1, keepdims=True), own_s)
    w = jnp.exp2((s - top) * LOG2_SCALE)
    own_w = jnp.exp2((own_s - top) * LOG2_SCALE)
    scale = 1.0 / (jnp.sum(w, axis=1, keepdims=True) + own_w)
    own_w = own_w.astype(jnp.bfloat16).astype(jnp.float32)
    for n in range(count):
        lines = slice(n * heads, (n + 1) * heads)
        mix = jnp.dot(
            w[lines].astype(jnp.bfloat16), cache[1, n], preferred_element_type=jnp.float32
        )
        picked = own_w[lines] * new_values[n]
        for kv in range(kv_heads):
            picked = picked + jnp.where(head_of == kv, mix[:, kv * D : (kv + 1) * D], 0.0)
        picked = picked * scale[lines]
        for head in range(heads):
            mixed[n : n + 1, head * D : (head + 1) * D] = picked[head : head + 1, :]
    out[...] = mixed[...].astype(out.dtype)


def finish_kernel(
    lengths, arrivals, own, first, second, third, *refs
):
    rows, (cache, tables, long_out, dec_out, mixed, held) = refs[:-6], refs[-6:]
    low = 0
    for block in rows:
        held[low : low + block.shape[0], :] = block[...]
        low += block.shape[0]
    decode(lengths, arrivals, (held, first, second, third), cache, tables, dec_out, mixed)
    combine(own, first, second, third, long_out)


def after(block, *others):
    return lax.optimization_barrier((block, *others))[0]


def exchange(block, axis, distance):
    count = lax.axis_size(axis)
    return lax.ppermute(block, axis, [(i, i ^ distance) for i in range(count)])


NEAR = pl.BlockSpec(memory_space=pltpu.VMEM)
FAR = pl.BlockSpec(memory_space=pltpu.MemorySpace.HBM)
def stay(*arrays):
    return [pltpu.with_memory_space_constraint(a, pltpu.MemorySpace.HBM) for a in arrays]


SCALARS = pl.BlockSpec(memory_space=pltpu.SMEM)


def shards(
    long_query,
    long_new_kv,
    sink_kv,
    window,
    long_len,
    long_offset,
    dec_query,
    dec_new_kv,
    dec_cache,
    dec_len,
    arrival_order,
):
    blk_count, head_count = lax.axis_size("blk"), lax.axis_size("head")
    rows, features = long_query.shape
    heads = features // D
    kv_width = long_new_kv.shape[2]
    kv_heads = kv_width // D
    group = heads // kv_heads
    slots = window.shape[1]
    members = SPAN // rows
    own_count = dec_cache.shape[1]

    queries = {part: exchange(long_query, "blk", part) for part in range(1, members)}

    half = jnp.arange(D, dtype=jnp.int32) % (D // 2)
    frequency = (10000.0 ** (-(half.astype(jnp.float32) * 2.0 / D))).reshape(1, D)

    def call(kernel, out_shape, operands, specs, scratch, aliases={}):
        return pl.pallas_call(
            kernel,
            in_specs=specs,
            out_specs=jax.tree.map(lambda _: NEAR, out_shape),
            out_shape=out_shape,
            scratch_shapes=scratch,
            input_output_aliases=aliases,
            compiler_params=VMEM,
        )(*operands)

    pieces = call(
        spread_kernel,
        (jax.ShapeDtypeStruct((PAD_PARTS, D), jnp.bfloat16),) * head_count,
        stay(dec_query, dec_new_kv),
        [FAR, FAR],
        [
            pltpu.VMEM(dec_query.shape, jnp.bfloat16),
            pltpu.VMEM(dec_new_kv.shape, jnp.bfloat16),
            pltpu.SemaphoreType.DMA((2,)),
        ],
    )
    arrived = jnp.concatenate(
        [exchange(piece, "head", r) if r else piece for r, piece in enumerate(pieces)], axis=0
    )
    total = slots + rows + D
    shared = call(
        prepare_kernel,
        (
            jax.ShapeDtypeStruct((total, kv_width), jnp.bfloat16),
            jax.ShapeDtypeStruct((kv_width, total), jnp.bfloat16),
            jax.ShapeDtypeStruct((members, rows, D), jnp.float32),
            jax.ShapeDtypeStruct((members, rows, D), jnp.float32),
            jax.ShapeDtypeStruct((members, total, rows), jnp.float32),
            jax.ShapeDtypeStruct((2, -(-own_count // 8) * 8, D), jnp.float32),
        ),
        (*stay(long_len, long_offset, long_new_kv, sink_kv, window, dec_len), frequency),
        [FAR] * 6 + [NEAR],
        [
            pltpu.SMEM(long_len.shape, jnp.int32),
            pltpu.SMEM(long_offset.shape, jnp.int32),
            pltpu.SMEM(dec_len.shape, jnp.int32),
            pltpu.VMEM(long_new_kv.shape, jnp.bfloat16),
            pltpu.VMEM((2, *sink_kv.shape[2:]), jnp.bfloat16),
            pltpu.VMEM(window.shape[1:], jnp.bfloat16),
            pltpu.VMEM((D, kv_width), jnp.float32),
            pltpu.SemaphoreType.DMA((7,)),
        ],
    )

    def attend(part, query, spare, *passenger):
        if part == 0:
            out = jax.ShapeDtypeStruct((features + heads, rows), jnp.float32)
        else:
            lines = features + LOG_LINES * heads + spare
            lines += sum(p.shape[0] for p in passenger)
            out = jax.ShapeDtypeStruct((lines, rows), jnp.bfloat16)
        return call(
            functools.partial(attend_kernel, part),
            out,
            (query, *shared[:5], *passenger),
            [NEAR] * (6 + len(passenger)),
            [
                pltpu.VMEM((kv_heads, total, group * rows), jnp.float32),
                pltpu.VMEM((kv_heads, total, group * rows), jnp.bfloat16),
            ],
        )

    arrived = after(arrived, shared[0])
    blocks, distance = [arrived], members
    while distance < blk_count:
        full = blocks[0] if len(blocks) == 1 else jnp.concatenate(blocks, axis=0)
        blocks = [full, exchange(full, "blk", distance)]
        distance *= 2
    spare = sum(block.shape[0] for block in blocks)
    mine = attend(0, long_query, 0)
    backs = {}
    for part in range(1, members):
        if part == members - 1:
            mix = attend(part, queries[part], spare)
            mix = call(
                append_kernel,
                jax.ShapeDtypeStruct(mix.shape, mix.dtype),
                (mix, *blocks),
                [NEAR] * (1 + len(blocks)),
                [],
                {0: 0},
            )
        else:
            mix = attend(part, queries[part], 0, *blocks)
        backs[part] = exchange(mix, "blk", part)
    first_back, second_back, third_back = [backs[part] for part in range(1, members)]
    return call(
        finish_kernel,
        (
            jax.ShapeDtypeStruct((rows, features), jnp.bfloat16),
            jax.ShapeDtypeStruct((own_count, features), jnp.bfloat16),
        ),
        (
            dec_len, arrival_order, mine, first_back, second_back, third_back,
            *blocks, dec_cache, shared[5],
        ),
        [SCALARS, SCALARS] + [NEAR] * (6 + len(blocks)),
        [
            pltpu.VMEM((own_count, features), jnp.float32),
            pltpu.VMEM((spare, D), jnp.bfloat16),
        ],
    )


def solution(mesh):
    in_specs = (
        P("blk", "head"),
        P(None, "blk", "head"),
        P(None, None, None, "head"),
        P(None, "blk", "head"),
        P(),
        P(),
        P(("blk", "head"), None),
        P(("blk", "head"), None, None),
        P(None, "blk", None, "head"),
        P("blk"),
        P(),
    )
    out_specs = (P("blk", "head"), P("blk", "head"))
    return jax.shard_map(shards, mesh=mesh, in_specs=in_specs, out_specs=out_specs, check_vma=False)
```
